256 devices in a mesh: group: 64 (over y_hi, x, z), tensor: 4 (over y_lo, core).
Axes of the slice: x: 4, y: 4 (y_hi: 2, y_lo: 2; y = y_hi * 2 + y_lo), z: 8, core: 2. Of those that a mesh axis runs over, the one named last changes fastest.
Arguments:
- master: float32 [8192, 8192], P(('group', 'tensor')), may hold values from -0.25 to 0.25
- states: bfloat16 [64, 128, 4096], P('group', None, 'tensor'), may hold values from -6 to 6
- norm_gain: float32 [8192], replicated, may hold values from 0.1 to 1.9
Outputs:
- decoded: bfloat16 [64, 128, 4096], P('group', None, 'tensor')
The draws below stay inside these ranges and needn't reach their ends.
All inputs are finite; a program needn't handle non-finite values.
Results may differ from the reference program's by a relative error of at most 0.0066.
Values may be sent and summed in bfloat16 or wider, within the bound.
No kernel may reach another device: no remote copies, remote signals or barrier semaphores. Data moves between devices by JAX's collectives and lax.ppermute only.
A program may use at most 128 MiB of HBM per device.

```python
import jax
import jax.numpy as jnp
from jax import lax

D = 8192
ROWS = 128
STEPS = 3
N_GROUP = 64
N_TENSOR = 4


def with_spikes(array, key, source, target, parts, factor):
    def block_of(position):
        return (jnp.arange(array.shape[position]) // (array.shape[position] // parts)).reshape((-1,) + (1,) * (array.ndim - 1 - position))

    first = jax.random.permutation(key, parts)[block_of(target)]
    second = (block_of(target) + parts // 2) % parts
    return jnp.where((block_of(source) == first) | (block_of(source) == second), factor * array, array)


def block_levels(stream_key, dims, split, low, top_value):
    gain = 1.0
    for axis_at, parts in split:
        draws = jax.random.uniform(jax.random.fold_in(jax.random.fold_in(stream_key, 6), axis_at), (parts,), jnp.float32, low / len(split), top_value / len(split))
        gain = gain * jnp.repeat(jnp.exp(draws), dims[axis_at] // parts).reshape((-1,) + (1,) * (len(dims) - 1 - axis_at))
    return gain


def normal_values(stream_key, shape, deviation, most, pieces=(), kind=jnp.bfloat16):
    array = deviation * jax.random.normal(stream_key, shape, jnp.float32)
    if pieces:
        array = array * block_levels(stream_key, shape, pieces, -0.22, 0.18)
    return jnp.clip(array, -most, most).astype(kind)


def bell_draw_with(own_key, shape, deviation, most, pieces, heavy, kind=jnp.bfloat16):
    array = deviation * jax.random.normal(own_key, shape, jnp.float32)
    if pieces:
        array = array * block_levels(own_key, shape, pieces, -0.22, 0.18)
    return jnp.clip(with_spikes(array, jax.random.fold_in(own_key, 3), *heavy), -most, most).astype(kind)


def setup_inputs(seed: int = 0) -> dict:
    seeds = jax.random.split(jax.random.key(seed), 4)
    return {
        "master": bell_draw_with(seeds[0], (D, D), D ** -0.5, 0.25, ((0, 256),), (0, 1, 256, 6.0), jnp.float32),
        "states": normal_values(seeds[1], (N_GROUP, ROWS, D // 2), 1.0, 6.0, ((0, 64), (2, 4))),
        "norm_gain": jnp.clip(1.0 + 0.18 * jax.random.normal(seeds[2], (D,), jnp.float32), 0.1, 1.9),
    }


epsilon = 1e-06

def reference(master, states, norm_gain):
    synced = master.astype(jnp.bfloat16)
    replicas = N_GROUP // 2
    block_width = D // (2 * N_TENSOR)
    split_view = states.reshape(replicas, 2, ROWS, N_TENSOR, block_width)
    current = jnp.transpose(split_view, (0, 2, 3, 1, 4)).reshape(replicas, ROWS, D)

    def one_replica(state_rows):
        for step_index in range(STEPS):
            widened = state_rows.astype(jnp.float32)
            inv_rms = lax.rsqrt(lax.optimization_barrier(jnp.mean(widened * widened, axis=1, keepdims=True)) + epsilon)
            normed = (widened * inv_rms * norm_gain).astype(jnp.bfloat16)
            product = jnp.dot(normed, synced, preferred_element_type=jnp.float32)
            state_rows = (widened + product).astype(jnp.bfloat16)
        return state_rows
    result = lax.map(one_replica, current)
    restored = result.reshape(replicas, ROWS, N_TENSOR, 2, block_width)
    restored = jnp.transpose(restored, (0, 3, 1, 2, 4)).reshape(N_GROUP, ROWS, D // 2)
    return restored
```

```python
import jax
import jax.numpy as jnp
from jax import lax
from jax.experimental import pallas as pl
from jax.experimental.pallas import tpu as pltpu
from jax.sharding import Mesh, PartitionSpec as P

D = 8192
EPS = 1e-06
STEPS = 3
NX, NZ = 4, 8
AXES = ("yh", "x", "zh", "z0", "yl", "c")
SIZES = (2, 4, 4, 2, 2, 2)
Y = ("yh", "yl")
Z = ("zh", "z0")
XZC = ("x", "z0", "c")
BF = jnp.bfloat16
F32 = jnp.float32


def xor_y(value, r):
    return lax.ppermute(value, Y, [(i, i ^ r) for i in range(4)])


def ring_z(value, step):
    return lax.ppermute(value, Z, [(i, (i + step) % NZ) for i in range(NZ)])


def other_core(value):
    return lax.ppermute(value, "c", [(0, 1), (1, 0)])


def first_kernel(lhs_ref, w_ref, out_ref):
    lhs = lhs_ref[...]
    for b in range(NX):
        part = jnp.dot(lhs, w_ref[:, b * 256 : (b + 1) * 256], preferred_element_type=F32)
        out_ref[b] = part.astype(BF)


def first_product(lhs, w):
    rows = lhs.shape[0]
    return pl.pallas_call(
        first_kernel,
        out_shape=jax.ShapeDtypeStruct((NX, rows, 256), BF),
        compiler_params=pltpu.CompilerParams(vmem_limit_bytes=48 << 20),
        cost_estimate=pl.CostEstimate(flops=2 * rows * 2048 * 1024, bytes_accessed=6 << 20, transcendentals=0),
        name="first_product",
    )(lhs, w)


def step_kernel(me_ref, p0, p1, p2, p3, w0, w1, out_ref, lhs):
    yl, yh = me_ref[0], me_ref[1]
    total = jnp.zeros((128, 1), F32)
    for r, piece in enumerate((p0, p1, p2, p3)):
        offset = (yl ^ (r & 1)) * 1024 + (yh ^ (r >> 1)) * 512
        value = piece[...]
        lhs[:, pl.ds(pl.multiple_of(offset, 512), 512)] = value
        wide = value.astype(F32)
        total = total + jnp.sum(wide * wide, axis=1, keepdims=True)
    across = jnp.transpose(jnp.broadcast_to(total, (128, 128)))[:16]
    upper = across.astype(BF).astype(F32)
    row = lax.broadcasted_iota(jnp.int32, (16, 128), 0)
    extra = jnp.where(row < 8, upper, across - upper).astype(BF)
    full = lhs[...]
    for b in range(NX):
        for n, w in enumerate((w0, w1)):
            part = jnp.dot(full, w[:, b * 256 : (b + 1) * 256], preferred_element_type=F32)
            out_ref[b, 0:128, n * 256 : (n + 1) * 256] = part.astype(BF)
        out_ref[b, 128:144, 0:128] = extra
        out_ref[b, 128:144, 128:512] = jnp.zeros((16, 384), BF)


def step_product(me, pieces, w):
    vmem = pl.BlockSpec(memory_space=pltpu.VMEM)
    return pl.pallas_call(
        step_kernel,
        out_shape=jax.ShapeDtypeStruct((NX, 144, 512), BF),
        in_specs=[pl.BlockSpec(memory_space=pltpu.SMEM)] + [vmem] * 6,
        out_specs=vmem,
        scratch_shapes=[pltpu.VMEM((128, 2048), BF)],
        compiler_params=pltpu.CompilerParams(vmem_limit_bytes=48 << 20),
        cost_estimate=pl.CostEstimate(flops=2 * 128 * 2048 * 2048, bytes_accessed=9 << 20, transcendentals=0),
        name="step_product",
    )(me, *pieces, *w)


def update_kernel(parts, h, out):
    square = jnp.zeros((8, 128), F32)
    for b in range(NX):
        extra = parts[b, 128:144, 0:128].astype(F32)
        square = square + extra[0:8] + extra[8:16]
    column = jnp.transpose(jnp.broadcast_to(square[0:1], (128, 128)))
    scale = lax.rsqrt(column * (1.0 / D) + EPS)
    for j in range(4):
        s = slice(j * 128, (j + 1) * 128)
        total = parts[0, 0:128, s].astype(F32) + parts[1, 0:128, s].astype(F32)
        total = total + (parts[2, 0:128, s].astype(F32) + parts[3, 0:128, s].astype(F32))
        out[:, s] = (h[:, s].astype(F32) + scale * total).astype(BF)


def update(parts, h):
    return pl.pallas_call(
        update_kernel,
        out_shape=jax.ShapeDtypeStruct((128, 512), BF),
        cost_estimate=pl.CostEstimate(flops=1 << 20, bytes_accessed=1 << 20, transcendentals=1 << 14),
        name="update",
    )(parts, h)


def per_device(master, states, norm_gain):
    yh, x, zh, z0, yl, c = (lax.axis_index(a) for a in AXES)
    z = zh * 2 + z0
    me = jnp.stack([yl, yh]).astype(jnp.int32)

    first_row = ((((yh * NX + x) * NZ + z) * 2 + yl) * 2 + c) * 32
    gain = lax.dynamic_slice_in_dim(norm_gain, first_row, 32)
    rounded = lax.reduce_precision(master, 8, 7)
    rows = (rounded * gain[:, None]).astype(BF)
    rows = rows.reshape(32, 2, NX, 2, 2, 256)
    w = []
    for n in range(2):
        send = jnp.transpose(rows[:, :, :, :, n], (3, 1, 0, 2, 4)).reshape(4, 32, 1024)
        own = lax.all_to_all(send, Y, split_axis=0, concat_axis=0, tiled=True).reshape(128, 1024)
        buf = jnp.zeros((2, NZ, 2, 2, 32, 1024), BF)

        def put(buf, piece, at):
            other = other_core(piece)
            a, b = piece.reshape(2, 1, 2, 1, 32, 1024), other.reshape(2, 1, 2, 1, 32, 1024)
            both = jnp.concatenate([jnp.where(c == 0, a, b), jnp.where(c == 0, b, a)], axis=3)
            return lax.dynamic_update_slice(buf, both, (0, at % NZ, 0, 0, 0, 0))

        buf = put(buf, own, z)
        right = left = own
        for d in range(1, 4):
            right, left = ring_z(right, 1), ring_z(left, -1)
            buf = put(buf, right, z - d + NZ)
            buf = put(buf, left, z + d)
        far = jnp.concatenate([ring_z(right[:64], 1), ring_z(left[64:], -1)], axis=0)
        buf = put(buf, far, z + 4)
        w.append(buf.reshape(2048, 1024))

    local = states[0].reshape(2, 2, 32, 1024)
    got = []
    for k in range(4):
        perm = []
        for i in range(16):
            sx, sz, sc = i >> 2, (i >> 1) & 1, i & 1
            v = sx ^ k
            perm.append((i, (sc * 2 + sz) * 4 + (v & 1) * 2 + (v >> 1)))
        v = x ^ k
        block = lax.dynamic_slice(local, (v & 1, v >> 1, 0, 0), (1, 1, 32, 1024))[0, 0]
        got.append(lax.ppermute(block, XZC, perm))
    got = jnp.stack(got)
    mine = c * 2 + z0
    placed = jnp.concatenate([lax.dynamic_slice_in_dim(got, mine ^ v, 1, 0) for v in range(4)], axis=0)
    gathered = lax.all_gather(placed, Y, axis=0, tiled=False)
    gathered = gathered.reshape(2, 2, 4, 2, 16, 1024)
    lhs = jnp.transpose(gathered, (3, 0, 2, 4, 1, 5)).reshape(256, 2048)
    h = lax.dynamic_slice_in_dim(lhs, yl * 1024 + yh * 512, 512, 1)
    wide = lhs.astype(F32)
    square = jnp.sum(wide * wide, axis=1)
    square = square + lax.ppermute(square, "x", [(i, i ^ 1) for i in range(4)])
    square = square + lax.ppermute(square, "x", [(i, i ^ 2) for i in range(4)])
    scale = lax.rsqrt(square * (1.0 / D) + EPS)[:, None]

    parts = []
    for n in range(2):
        send = first_product(lhs, w[n])
        back = lax.all_to_all(send, "x", split_axis=0, concat_axis=0, tiled=True)
        parts.append(jnp.sum(back.astype(F32), axis=0))
    h = (h.astype(F32) + scale * jnp.concatenate(parts, axis=1)).astype(BF)

    halves = [h[:128], h[128:]]
    for _ in range(1, STEPS):
        for i in range(2):
            h = halves[i]
            pieces = [h] + [xor_y(h, r) for r in (1, 2, 3)]
            send = step_product(me, pieces, w)
            back = lax.all_to_all(send, "x", split_axis=0, concat_axis=0, tiled=True)
            halves[i] = update(back, h)

    out = []
    for h in halves:
        h = h.reshape(2, 64, 512)
        keep = lax.dynamic_slice_in_dim(h, yh, 1, 0)[0]
        give = lax.dynamic_slice_in_dim(h, 1 - yh, 1, 0)[0]
        take = lax.ppermute(give, "yh", [(0, 1), (1, 0)])
        full = jnp.concatenate([jnp.where(yh == 0, keep, take), jnp.where(yh == 0, take, keep)], axis=1)
        full = full.reshape(4, 16, 1024)
        got = []
        for k in range(4):
            perm = []
            for i in range(16):
                sx, sz, sc = i >> 2, (i >> 1) & 1, i & 1
                perm.append((i, ((sc * 2 + sz) ^ k) * 4 + (sx & 1) * 2 + (sx >> 1)))
            block = lax.dynamic_slice_in_dim(full, mine ^ k, 1, 0)[0]
            got.append(lax.ppermute(block, XZC, perm))
        got = jnp.stack(got)
        out.append(jnp.concatenate([lax.dynamic_slice_in_dim(got, x ^ v, 1, 0) for v in (0, 2, 1, 3)], axis=0))
    result = jnp.stack(out, axis=1).reshape(128, 1024)
    return result[None]


def solution(mesh):
    fine = Mesh(mesh.devices.reshape(SIZES), AXES)
    group = AXES[:4]
    in_specs = (P(AXES, None), P(group, None, AXES[4:]), P())
    out_specs = P(group, None, AXES[4:])
    return jax.shard_map(per_device, mesh=fine, in_specs=in_specs, out_specs=out_specs, check_vma=False)
```

```python
import functools

import jax
import jax.numpy as jnp
from jax import lax
from jax.experimental import pallas as pl
from jax.experimental.pallas import tpu as pltpu
from jax.sharding import Mesh, PartitionSpec as P

D = 8192
EPS = 1e-06
STEPS = 3
NX, NZ = 4, 8
HALF = 256
WIDE = 256
AXES = ("yh", "x", "zh", "z0", "yl", "c")
SIZES = (2, 4, 4, 2, 2, 2)
Y = ("yh", "yl")
Z = ("zh", "z0")
YC = ("yh", "yl", "c")
XZC = ("x", "z0", "c")
BF = jnp.bfloat16
F32 = jnp.float32
VMEM = pl.BlockSpec(memory_space=pltpu.VMEM)
SMEM = pl.BlockSpec(memory_space=pltpu.SMEM)
PARAMS = pltpu.CompilerParams(vmem_limit_bytes=12 << 20)


def xor_y(value, r):
    return lax.ppermute(value, Y, [(i, i ^ r) for i in range(4)])


def xor_x(value, r):
    return lax.ppermute(value, "x", [(i, i ^ r) for i in range(4)])


def ring_z(value, step):
    return lax.ppermute(value, Z, [(i, (i + step) % NZ) for i in range(NZ)])


def other_core(value):
    return lax.ppermute(value, "c", [(0, 1), (1, 0)])


def cut_kernel(at_ref, master, gain, out, column):
    row = gain[pl.ds(at_ref[0], 1), :]
    column[...] = jnp.transpose(jnp.broadcast_to(row, (128, 128)))
    scale = column[pl.ds(pl.multiple_of(at_ref[1], 32), 32), :]
    scale = jnp.concatenate([scale, scale], axis=1)
    for b12 in range(2):
        for xx in range(NX):
            for b9 in range(2):
                for b8 in range(2):
                    f = b12 * 4096 + xx * 1024 + b9 * 512 + b8 * 256
                    rounded = master[:, f : f + 256].astype(BF).astype(F32)
                    out[b9 * 4 + b12 * 2 + b8, :, xx * 256 : (xx + 1) * 256] = (rounded * scale).astype(BF)


def cut(at, master, gain):
    return pl.pallas_call(
        cut_kernel,
        out_shape=jax.ShapeDtypeStruct((8, 32, 1024), BF),
        in_specs=[SMEM, VMEM, VMEM],
        out_specs=VMEM,
        scratch_shapes=[pltpu.VMEM((128, 128), F32)],
        compiler_params=PARAMS,
        name="cut",
    )(at, master, gain.reshape(64, 128))


def squares_to_rows(sums):
    row = []
    for j in range(2):
        tile = jnp.transpose(sums[j * 128 : (j + 1) * 128])
        row.append(jnp.broadcast_to(jnp.sum(tile, axis=0, keepdims=True), (16, 128)))
    row = jnp.concatenate(row, axis=1)
    upper = row.astype(BF).astype(F32)
    at = lax.broadcasted_iota(jnp.int32, (16, 256), 0)
    return jnp.where(at < 8, upper, row - upper).astype(BF)


def lane_sums(value):
    wide = value.astype(F32)
    wide = wide * wide
    total = wide[:, 0:128]
    for j in range(1, value.shape[1] // 128):
        total = total + wide[:, j * 128 : (j + 1) * 128]
    return total


def build_kernel(me_ref, *refs):
    pieces, lhs, extra, sums = refs[:8], refs[8], refs[9], refs[10]
    yl, yh, c = me_ref[0], me_ref[1], me_ref[2]
    for i, piece in enumerate(pieces):
        r, far = i % 4, i // 4
        at = (yh ^ (r >> 1)) * 512 + (c ^ far) * 256
        value = piece[...]
        lhs[yl ^ (r & 1), :, pl.ds(pl.multiple_of(at, 256), 256)] = value
        if i == 0:
            sums[...] = lane_sums(value)
        else:
            sums[...] += lane_sums(value)
    extra[...] = squares_to_rows(sums[...])


def build(me, pieces):
    return pl.pallas_call(
        build_kernel,
        out_shape=[jax.ShapeDtypeStruct((2, HALF, 1024), BF), jax.ShapeDtypeStruct((16, WIDE), BF)],
        in_specs=[SMEM] + [VMEM] * 8,
        out_specs=[VMEM, VMEM],
        scratch_shapes=[pltpu.VMEM((HALF, 128), F32)],
        compiler_params=PARAMS,
        name="build",
    )(me, *pieces)


def first_build_kernel(me_ref, own, other, lhs, extra, h, sums):
    yl, yh, c, z0 = me_ref[0], me_ref[1], me_ref[2], me_ref[4]
    for r in range(4):
        for far, piece in enumerate((own, other)):
            for k in range(4):
                at = (yh ^ (r >> 1)) * 128 + (((c ^ far) * 2 + z0) ^ k) * 32
                lhs[c ^ far, yl ^ (r & 1), pl.ds(pl.multiple_of(at, 32), 32), :] = piece[r, k]
    for m in range(2):
        sums[...] = lane_sums(lhs[m, 0]) + lane_sums(lhs[m, 1])
        extra[m] = squares_to_rows(sums[...])
        h[m] = lhs[m, yl, :, pl.ds(pl.multiple_of(yh * 512 + c * 256, 256), 256)]


def first_build(me, own, other):
    return pl.pallas_call(
        first_build_kernel,
        out_shape=[
            jax.ShapeDtypeStruct((2, 2, HALF, 1024), BF),
            jax.ShapeDtypeStruct((2, 16, WIDE), BF),
            jax.ShapeDtypeStruct((2, HALF, WIDE), BF),
        ],
        in_specs=[SMEM, VMEM, VMEM],
        out_specs=[VMEM, VMEM, VMEM],
        scratch_shapes=[pltpu.VMEM((HALF, 128), F32)],
        compiler_params=PARAMS,
        name="first_build",
    )(me, own, other)


def product_kernel(half, me_ref, lhs, extra, w0, w1, *outs):
    for r in (2, 1, 3, 0):
        cols = pl.ds(pl.multiple_of((me_ref[3] ^ r) * WIDE, WIDE), WIDE)
        left, right = (lhs[0], lhs[1]) if half is None else (lhs[half, 0], lhs[half, 1])
        part = jnp.dot(left, w0[:, cols], preferred_element_type=F32)
        part = part + jnp.dot(right, w1[:, cols], preferred_element_type=F32)
        outs[r][0:HALF, :] = part.astype(BF)
        outs[r][HALF : HALF + 16, :] = extra[...] if half is None else extra[half]


def product(me, lhs, extra, w, half=None):
    return pl.pallas_call(
        functools.partial(product_kernel, half),
        out_shape=[jax.ShapeDtypeStruct((HALF + 16, WIDE), BF)] * 4,
        in_specs=[SMEM] + [VMEM] * 4,
        out_specs=[VMEM] * 4,
        compiler_params=PARAMS,
        cost_estimate=pl.CostEstimate(flops=2 * HALF * 2048 * 1024, bytes_accessed=6 << 20, transcendentals=0),
        name="product",
    )(me, lhs, extra, *w)


def update_kernel(h, p0, p1, p2, p3, out):
    parts = (p0, p1, p2, p3)
    for j in range(2):
        rows, lanes = slice(j * 128, (j + 1) * 128), slice(j * 128, (j + 1) * 128)
        square = jnp.zeros((8, 128), F32)
        for part in parts:
            extra = part[HALF : HALF + 16, lanes].astype(F32)
            square = square + extra[0:8] + extra[8:16]
        scale = lax.rsqrt(jnp.transpose(jnp.broadcast_to(square[0:1], (128, 128))) * (1.0 / D) + EPS)
        scale = jnp.concatenate([scale, scale], axis=1)
        total = p0[rows, :].astype(F32) + p1[rows, :].astype(F32)
        total = total + (p2[rows, :].astype(F32) + p3[rows, :].astype(F32))
        out[rows, :] = (h[rows, :].astype(F32) + scale * total).astype(BF)


def update(h, parts):
    return pl.pallas_call(
        update_kernel,
        out_shape=jax.ShapeDtypeStruct((HALF, WIDE), BF),
        in_specs=[VMEM] * 5,
        out_specs=VMEM,
        compiler_params=PARAMS,
        name="update",
    )(h, *parts)


def place_kernel(me_ref, *refs):
    out = refs[8]
    for i, block in enumerate(refs[:8]):
        half, v = i // 4, me_ref[3] ^ (i % 4)
        row = pl.ds(pl.multiple_of((v & 1) * 64 + half * 32, 32), 32)
        for s in range(2):
            out[row, pl.ds(pl.multiple_of(s * 512 + (v >> 1) * 256, 256), 256)] = block[s]


def place(me, blocks):
    return pl.pallas_call(
        place_kernel,
        out_shape=jax.ShapeDtypeStruct((128, 1024), BF),
        in_specs=[SMEM] + [VMEM] * 8,
        out_specs=VMEM,
        compiler_params=PARAMS,
        name="place",
    )(me, *blocks)


def swap_x_with_zc(k, back):
    perm = []
    for i in range(16):
        x, z0, c = i >> 2, (i >> 1) & 1, i & 1
        v = x ^ k
        perm.append((i, (c * 2 + z0) * 4 + (v & 1) * 2 + (v >> 1)))
    return [(b, a) for a, b in perm] if back else perm


def per_device(master, states, norm_gain):
    yh, x, zh, z0, yl, c = (lax.axis_index(a).astype(jnp.int32) for a in AXES)
    z = zh * 2 + z0
    mine = c * 2 + z0
    me = jnp.stack([yl, yh, c, x, z0])
    row_block = (((yh * NX + x) * NZ + z) * 2 + yl) * 2 + c

    send = cut(jnp.stack([row_block // 4, row_block % 4 * 32]), master, norm_gain)
    own = lax.all_to_all(send, YC, split_axis=0, concat_axis=0, tiled=True).reshape(2, 128, 1024)
    w = []
    for n in range(2):
        piece = own[n]
        buf = jnp.zeros((NZ, 128, 1024), BF)

        def put(buf, piece, at):
            return lax.dynamic_update_slice(buf, piece[None], (at % NZ, 0, 0))

        buf = put(buf, piece, z)
        right = left = piece
        for d in range(1, 4):
            right, left = ring_z(right, 1), ring_z(left, -1)
            if n == 0 and d == 1:
                right, states = lax.optimization_barrier((right, states))
            buf = put(buf, right, z - d + NZ)
            buf = put(buf, left, z + d)
        buf = lax.dynamic_update_slice(buf, ring_z(right[:64], 1)[None], ((z + 4) % NZ, 0, 0))
        buf = lax.dynamic_update_slice(buf, ring_z(left[64:], -1)[None], ((z + 4) % NZ, 64, 0))
        w.append(buf.reshape(1024, 1024))

    local = states[0].reshape(2, 2, 32, 1024)
    got = []
    for k in range(4):
        v = x ^ k
        block = lax.dynamic_slice(local, (v & 1, v >> 1, 0, 0), (1, 1, 32, 1024))[0, 0]
        got.append(lax.ppermute(block, XZC, swap_x_with_zc(k, False)))
    got = jnp.stack(got)
    got = jnp.stack([got] + [xor_y(got, r) for r in (1, 2, 3)])
    lhs, extra, h = first_build(me, got, other_core(got))

    halves = [h[0], h[1]]

    def gather(h):
        pieces = [h] + [xor_y(h, r) for r in (1, 2, 3)]
        return build(me, pieces + [other_core(p) for p in pieces])

    def reduce(h, send):
        return update(h, [send[0]] + [xor_x(send[r], r) for r in (1, 2, 3)])

    sends = [product(me, lhs, extra, w, half) for half in range(2)]
    for step in range(STEPS):
        for half in range(2):
            halves[half] = reduce(halves[half], sends[half])
            if step + 1 < STEPS:
                sends[half] = product(me, *gather(halves[half]), w)

    blocks = []
    for h in halves:
        h = h.reshape(2, 4, 32, WIDE)
        keep = lax.dynamic_index_in_dim(h, yh, 0, keepdims=False)
        take = lax.ppermute(lax.dynamic_index_in_dim(h, 1 - yh, 0, keepdims=False), "yh", [(0, 1), (1, 0)])
        h = jnp.stack([jnp.where(yh == 0, keep, take), jnp.where(yh == 0, take, keep)], axis=1)
        for k in range(4):
            block = lax.dynamic_index_in_dim(h, mine ^ k, 0, keepdims=False)
            blocks.append(lax.ppermute(block, XZC, swap_x_with_zc(k, True)))
    return place(me, blocks)[None]


def solution(mesh):
    fine = Mesh(mesh.devices.reshape(SIZES), AXES)
    group = AXES[:4]
    in_specs = (P(AXES, None), P(group, None, AXES[4:]), P())
    out_specs = P(group, None, AXES[4:])
    return jax.shard_map(per_device, mesh=fine, in_specs=in_specs, out_specs=out_specs, check_vma=False)
```

```python
import functools

import jax
import jax.numpy as jnp
from jax import lax
from jax.experimental import pallas as pl
from jax.experimental.pallas import tpu as pltpu
from jax.sharding import Mesh, PartitionSpec as P

D = 8192
EPS = 1e-06
STEPS = 3
NX, NZ = 4, 8
HALF = 256
WIDE = 256
AXES = ("yh", "x", "zh", "z0", "yl", "c")
SIZES = (2, 4, 4, 2, 2, 2)
Y = ("yh", "yl")
Z = ("zh", "z0")
YC = ("yh", "yl", "c")
XZC = ("x", "z0", "c")
BF = jnp.bfloat16
F32 = jnp.float32
VMEM = pl.BlockSpec(memory_space=pltpu.VMEM)
SMEM = pl.BlockSpec(memory_space=pltpu.SMEM)
PARAMS = pltpu.CompilerParams(vmem_limit_bytes=12 << 20)


def xor_y(value, r):
    return lax.ppermute(value, Y, [(i, i ^ r) for i in range(4)])


def xor_x(value, r):
    return lax.ppermute(value, "x", [(i, i ^ r) for i in range(4)])


def ring_z(value, step):
    return lax.ppermute(value, Z, [(i, (i + step) % NZ) for i in range(NZ)])


def tie(a, b):
    return lax.optimization_barrier((a, b))


def other_core(value):
    return lax.ppermute(value, "c", [(0, 1), (1, 0)])


def cut_kernel(at_ref, master, gain, out, column):
    row = gain[pl.ds(at_ref[0], 1), :]
    column[...] = jnp.transpose(jnp.broadcast_to(row, (128, 128)))
    scale = column[pl.ds(pl.multiple_of(at_ref[1], 32), 32), :]
    scale = jnp.concatenate([scale, scale], axis=1)
    for b12 in range(2):
        for xx in range(NX):
            for b9 in range(2):
                for b8 in range(2):
                    f = b12 * 4096 + xx * 1024 + b9 * 512 + b8 * 256
                    value = (master[:, f : f + 256].astype(BF).astype(F32) * scale).astype(BF)
                    out[b9 * 4 + b12 * 2 + b8, :, xx * 128 : (xx + 1) * 128] = value[:, :128]
                    out[b9 * 4 + b12 * 2 + b8, :, 512 + xx * 128 : 512 + (xx + 1) * 128] = value[:, 128:]


def cut(at, master, gain):
    return pl.pallas_call(
        cut_kernel,
        out_shape=jax.ShapeDtypeStruct((8, 32, 1024), BF),
        in_specs=[SMEM, VMEM, VMEM],
        out_specs=VMEM,
        scratch_shapes=[pltpu.VMEM((128, 128), F32)],
        compiler_params=PARAMS,
        name="cut",
    )(at, master, gain.reshape(64, 128))


def squares_to_rows(sums):
    row = []
    for j in range(2):
        tile = jnp.transpose(sums[j * 128 : (j + 1) * 128])
        row.append(jnp.broadcast_to(jnp.sum(tile, axis=0, keepdims=True), (16, 128)))
    row = jnp.concatenate(row, axis=1)
    upper = row.astype(BF).astype(F32)
    at = lax.broadcasted_iota(jnp.int32, (16, 256), 0)
    return jnp.where(at < 8, upper, row - upper).astype(BF)


def lane_sums(value):
    wide = value.astype(F32)
    wide = wide * wide
    total = wide[:, 0:128]
    for j in range(1, value.shape[1] // 128):
        total = total + wide[:, j * 128 : (j + 1) * 128]
    return total


def build_kernel(me_ref, *refs):
    pieces, lhs, extra, sums = refs[:8], refs[8], refs[9], refs[10]
    yl, yh, c = me_ref[0], me_ref[1], me_ref[2]
    for half in range(2):
        rows = slice(half * HALF, (half + 1) * HALF)
        total = jnp.zeros((HALF, 128), F32)
        for i, piece in enumerate(pieces):
            r, far = i % 4, i // 4
            at = (yh ^ (r >> 1)) * 512 + (c ^ far) * 256
            value = piece[rows, :]
            lhs[half, yl ^ (r & 1), :, pl.ds(pl.multiple_of(at, 256), 256)] = value
            total = total + lane_sums(value)
        sums[...] = total
        extra[half] = squares_to_rows(sums[...])


def build(me, pieces):
    return pl.pallas_call(
        build_kernel,
        out_shape=[jax.ShapeDtypeStruct((2, 2, HALF, 1024), BF), jax.ShapeDtypeStruct((2, 16, WIDE), BF)],
        in_specs=[SMEM] + [VMEM] * 8,
        out_specs=[VMEM, VMEM],
        scratch_shapes=[pltpu.VMEM((HALF, 128), F32)],
        compiler_params=PARAMS,
        name="build",
    )(me, *pieces)


def first_build_kernel(me_ref, own, other, lhs, extra, h, sums):
    yl, yh, c, z0 = me_ref[0], me_ref[1], me_ref[2], me_ref[4]
    for r in range(4):
        for far, piece in enumerate((own, other)):
            for k in range(4):
                at = (yh ^ (r >> 1)) * 128 + (((c ^ far) * 2 + z0) ^ k) * 32
                lhs[c ^ far, yl ^ (r & 1), pl.ds(pl.multiple_of(at, 32), 32), :] = piece[r, k]
    for m in range(2):
        sums[...] = lane_sums(lhs[m, 0]) + lane_sums(lhs[m, 1])
        extra[m] = squares_to_rows(sums[...])
        h[m] = lhs[m, yl, :, pl.ds(pl.multiple_of(yh * 512 + c * 256, 256), 256)]


def first_build(me, own, other):
    return pl.pallas_call(
        first_build_kernel,
        out_shape=[
            jax.ShapeDtypeStruct((2, 2, HALF, 1024), BF),
            jax.ShapeDtypeStruct((2, 16, WIDE), BF),
            jax.ShapeDtypeStruct((2, HALF, WIDE), BF),
        ],
        in_specs=[SMEM, VMEM, VMEM],
        out_specs=[VMEM, VMEM, VMEM],
        scratch_shapes=[pltpu.VMEM((HALF, 128), F32)],
        compiler_params=PARAMS,
        name="first_build",
    )(me, own, other)


def multiply(left, right, w):
    part = jnp.dot(left, w[:1024, :], preferred_element_type=F32)
    return part + jnp.dot(right, w[1024:, :], preferred_element_type=F32)


def first_product_kernel(me_ref, lhs, extra, w, *refs):
    outs, full = refs[:4], refs[4]
    for half in range(2):
        full[...] = multiply(lhs[half, 0], lhs[half, 1], w)
        for r in range(4):
            cols = pl.ds(pl.multiple_of((me_ref[3] ^ r) * 128, 128), 128)
            outs[r][half * HALF : (half + 1) * HALF, :] = full[:, cols].astype(BF)
    if outs[0].shape[0] > 2 * HALF:
        for r in range(4):
            for half in range(2):
                for j in range(2):
                    at = 2 * HALF + half * 32 + j * 16
                    outs[r][at : at + 16, :] = extra[half, :, j * 128 : (j + 1) * 128]


def first_product(me, lhs, extra, w, n):
    return pl.pallas_call(
        first_product_kernel,
        out_shape=[jax.ShapeDtypeStruct((2 * HALF + (0 if n else 64), 128), BF)] * 4,
        in_specs=[SMEM] + [VMEM] * 3,
        out_specs=[VMEM] * 4,
        scratch_shapes=[pltpu.VMEM((HALF, 512), F32)],
        compiler_params=PARAMS,
        cost_estimate=pl.CostEstimate(flops=1, bytes_accessed=1, transcendentals=0),
        name="first_product",
    )(me, lhs, extra, w)


def first_update_kernel(n, h, *refs):
    parts, sums, out = refs[:4], refs[4:8], refs[8]
    for half in range(2):
        for j in range(2):
            rows = slice(half * HALF + j * 128, half * HALF + (j + 1) * 128)
            at = 2 * HALF + half * 32 + j * 16
            square = jnp.zeros((8, 128), F32)
            for part in sums:
                extra = part[at : at + 16, :].astype(F32)
                square = square + extra[0:8] + extra[8:16]
            scale = lax.rsqrt(jnp.transpose(jnp.broadcast_to(square[0:1], (128, 128))) * (1.0 / D) + EPS)
            total = parts[0][rows, :].astype(F32) + parts[1][rows, :].astype(F32)
            total = total + (parts[2][rows, :].astype(F32) + parts[3][rows, :].astype(F32))
            old = h[half, j * 128 : (j + 1) * 128, n * 128 : (n + 1) * 128].astype(F32)
            out[rows, :] = (old + scale * total).astype(BF)


def first_update(h, parts, sums, n):
    return pl.pallas_call(
        functools.partial(first_update_kernel, n),
        out_shape=jax.ShapeDtypeStruct((2 * HALF, 128), BF),
        in_specs=[VMEM] * 9,
        out_specs=VMEM,
        compiler_params=PARAMS,
        name="first_update",
    )(h, *parts, *sums)


def second_build_kernel(me_ref, *refs):
    pieces, lhs, extra, h, sums = refs[:16], refs[16], refs[17], refs[18], refs[19]
    yl, yh, c = me_ref[0], me_ref[1], me_ref[2]
    for half in range(2):
        rows = slice(half * HALF, (half + 1) * HALF)
        total = jnp.zeros((HALF, 128), F32)
        for i, piece in enumerate(pieces):
            n, far, r = i // 8, i // 4 % 2, i % 4
            at = (yh ^ (r >> 1)) * 512 + (c ^ far) * 256 + n * 128
            value = piece[rows, :]
            lhs[half, yl ^ (r & 1), :, pl.ds(pl.multiple_of(at, 128), 128)] = value
            total = total + lane_sums(value)
            if i % 8 == 0:
                h[half, :, n * 128 : (n + 1) * 128] = value
        sums[...] = total
        extra[half] = squares_to_rows(sums[...])


def second_build(me, pieces):
    return pl.pallas_call(
        second_build_kernel,
        out_shape=[
            jax.ShapeDtypeStruct((2, 2, HALF, 1024), BF),
            jax.ShapeDtypeStruct((2, 16, WIDE), BF),
            jax.ShapeDtypeStruct((2, HALF, WIDE), BF),
        ],
        in_specs=[SMEM] + [VMEM] * 16,
        out_specs=[VMEM] * 3,
        scratch_shapes=[pltpu.VMEM((HALF, 128), F32)],
        compiler_params=PARAMS,
        name="second_build",
    )(me, *pieces)


def product_kernel(r, me_ref, lhs, extra, w0, w1, out):
    cols = pl.ds(pl.multiple_of((me_ref[3] ^ r) * 128, 128), 128)
    both = [jnp.concatenate([w0[k : k + 1024, cols], w1[k : k + 1024, cols]], axis=1) for k in (0, 1024)]
    for half in range(2):
        part = jnp.dot(lhs[half, 0], both[0], preferred_element_type=F32)
        part = part + jnp.dot(lhs[half, 1], both[1], preferred_element_type=F32)
        out[half * HALF : (half + 1) * HALF, :] = part.astype(BF)
        out[2 * HALF + half * 16 : 2 * HALF + half * 16 + 16, :] = extra[half]


def product(me, lhs, extra, w):
    outs = {}
    for r in (2, 1, 3, 0):
        outs[r] = pl.pallas_call(
            functools.partial(product_kernel, r),
            out_shape=jax.ShapeDtypeStruct((2 * HALF + 32, WIDE), BF),
            in_specs=[SMEM] + [VMEM] * 4,
            out_specs=VMEM,
            compiler_params=PARAMS,
            cost_estimate=pl.CostEstimate(flops=1, bytes_accessed=1, transcendentals=0),
            name="product",
        )(me, lhs, extra, *w)
    return outs


def last_product_kernel(me_ref, lhs, w0, w1, *refs):
    outs, full, sums = refs[:4], refs[4], refs[5]
    for half in range(2):
        for n, w in enumerate((w0, w1)):
            full[half, :, n * 512 : (n + 1) * 512] = multiply(lhs[half, 0], lhs[half, 1], w).astype(BF)
        sums[half] = lane_sums(lhs[half, 0]) + lane_sums(lhs[half, 1])
    for r in range(4):
        squares = []
        for m in range(2):
            for half in range(2):
                rows = pl.ds(pl.multiple_of(m * 128 + (me_ref[3] ^ r) * 32, 32), 32)
                at = m * 64 + half * 32
                outs[r][at : at + 32, :] = full[half, rows, :]
                squares.append(sums[half, rows, :])
        tile = jnp.transpose(jnp.concatenate(squares, axis=0))
        row = jnp.broadcast_to(jnp.sum(tile, axis=0, keepdims=True), (16, 128))
        upper = row.astype(BF).astype(F32)
        at = lax.broadcasted_iota(jnp.int32, (16, 128), 0)
        outs[r][128:144, 0:128] = jnp.where(at < 8, upper, row - upper).astype(BF)
        outs[r][128:144, 128:1024] = jnp.zeros((16, 896), BF)


def last_product(me, lhs, w):
    return pl.pallas_call(
        last_product_kernel,
        out_shape=[jax.ShapeDtypeStruct((144, 1024), BF)] * 4,
        in_specs=[SMEM] + [VMEM] * 3,
        out_specs=[VMEM] * 4,
        scratch_shapes=[pltpu.VMEM((2, HALF, 1024), BF), pltpu.VMEM((2, HALF, 128), F32)],
        compiler_params=PARAMS,
        cost_estimate=pl.CostEstimate(flops=1, bytes_accessed=1, transcendentals=0),
        name="last_product",
    )(me, lhs, *w)


def scale_of(parts, at, lane):
    square = jnp.zeros((8, 128), F32)
    for part in parts:
        extra = part[at : at + 16, lane : lane + 128].astype(F32)
        square = square + extra[0:8] + extra[8:16]
    return lax.rsqrt(jnp.transpose(jnp.broadcast_to(square[0:1], (128, 128))) * (1.0 / D) + EPS)


def add_up(parts, rows, cols):
    total = parts[0][rows, cols].astype(F32) + parts[1][rows, cols].astype(F32)
    return total + (parts[2][rows, cols].astype(F32) + parts[3][rows, cols].astype(F32))


def update_kernel(h, p0, p1, p2, p3, out):
    parts = (p0, p1, p2, p3)
    for j in range(4):
        rows = slice(j * 128, (j + 1) * 128)
        scale = scale_of(parts, 2 * HALF + (j // 2) * 16, (j % 2) * 128)
        for n in range(2):
            cols = slice(n * 128, (n + 1) * 128)
            out[rows, cols] = (h[rows, cols].astype(F32) + scale * add_up(parts, rows, cols)).astype(BF)


def update(h, parts):
    return pl.pallas_call(
        update_kernel,
        out_shape=jax.ShapeDtypeStruct((2 * HALF, WIDE), BF),
        in_specs=[VMEM] * 5,
        out_specs=VMEM,
        compiler_params=PARAMS,
        name="update",
    )(h, *parts)


def rows_by_x_kernel(me_ref, h, *outs):
    for r in range(4):
        for m in range(2):
            for half in range(2):
                rows = pl.ds(pl.multiple_of(half * HALF + m * 128 + (me_ref[3] ^ r) * 32, 32), 32)
                at = m * 64 + half * 32
                outs[r][at : at + 32, :] = h[rows, :]


def rows_by_x(me, h):
    return pl.pallas_call(
        rows_by_x_kernel,
        out_shape=[jax.ShapeDtypeStruct((128, WIDE), BF)] * 4,
        in_specs=[SMEM, VMEM],
        out_specs=[VMEM] * 4,
        compiler_params=PARAMS,
        name="rows_by_x",
    )(me, h)


def last_update_kernel(me_ref, *refs):
    parts, old, outs = refs[:4], refs[4:8], refs[8]
    yh, c, x, z0 = me_ref[1], me_ref[2], me_ref[3], me_ref[4]
    scale = scale_of(parts, 128, 0)
    for r in range(4):
        xx = x ^ r
        for n in range(2):
            cols = pl.ds(pl.multiple_of(n * 512 + xx * 128, 128), 128)
            value = old[r][:, n * 128 : (n + 1) * 128].astype(F32) + scale * add_up(parts, slice(0, 128), cols)
            for m in range(2):
                to = (m ^ yh) * 2 + ((xx & 1) ^ z0)
                outs[to, (xx >> 1) ^ c, :, n * 128 : (n + 1) * 128] = value[m * 64 : (m + 1) * 64].astype(BF)


def last_update(me, parts, old):
    return pl.pallas_call(
        last_update_kernel,
        out_shape=jax.ShapeDtypeStruct((4, 2, 64, WIDE), BF),
        in_specs=[SMEM] + [VMEM] * 8,
        out_specs=VMEM,
        compiler_params=PARAMS,
        name="last_update",
    )(me, *parts, *old)


def place_kernel(me_ref, *refs):
    out = refs[8]
    yh, c, z0 = me_ref[1], me_ref[2], me_ref[4]
    for i, block in enumerate(refs[:8]):
        far, dy, dz = i // 4, i // 2 % 2, i % 2
        row = pl.ds(pl.multiple_of((z0 ^ dz) * 64, 64), 64)
        col = pl.ds(pl.multiple_of((yh ^ dy) * 512 + (c ^ far) * 256, 256), 256)
        out[row, col] = block[0] if far == 0 else block[...]


def place(me, blocks):
    return pl.pallas_call(
        place_kernel,
        out_shape=jax.ShapeDtypeStruct((128, 1024), BF),
        in_specs=[SMEM] + [VMEM] * 8,
        out_specs=VMEM,
        compiler_params=PARAMS,
        name="place",
    )(me, *blocks)


def swap_x_with_zc(k):
    perm = []
    for i in range(16):
        x, z0, c = i >> 2, (i >> 1) & 1, i & 1
        v = x ^ k
        perm.append((i, (c * 2 + z0) * 4 + (v & 1) * 2 + (v >> 1)))
    return perm


def per_device(master, states, norm_gain):
    yh, x, zh, z0, yl, c = (lax.axis_index(a).astype(jnp.int32) for a in AXES)
    z = zh * 2 + z0
    mine = c * 2 + z0
    me = jnp.stack([yl, yh, c, x, z0])
    row_block = (((yh * NX + x) * NZ + z) * 2 + yl) * 2 + c

    send = cut(jnp.stack([row_block // 4, row_block % 4 * 32]), master, norm_gain)
    own = lax.all_to_all(send, YC, split_axis=0, concat_axis=0, tiled=True).reshape(256, 1024)
    w, early = [], None
    for n in range(2):
        piece = own[:, n * 512 : (n + 1) * 512]
        buf = jnp.zeros((2, NZ, 128, 512), BF)

        def put(buf, piece, at, part=0):
            return lax.dynamic_update_slice(buf, piece.reshape(-1, 1, 128, 512), (part, at % NZ, 0, 0))

        buf = put(buf, piece, z)
        right = left = piece
        for d in range(1, 4):
            right, left = ring_z(right, 1), ring_z(left, -1)
            early = right if early is None else early
            buf = put(buf, right, z - d + NZ)
            buf = put(buf, left, z + d)
        buf = put(buf, ring_z(right[:128], 1), z + 4, 0)
        buf = put(buf, ring_z(left[128:], -1), z + 4, 1)
        w.append(buf.reshape(2048, 512))

    local = states[0].reshape(2, 2, 32, 1024)
    got = []
    for k in range(4):
        v = x ^ k
        block = lax.dynamic_slice(local, (v & 1, v >> 1, 0, 0), (1, 1, 32, 1024))[0, 0]
        got.append(lax.ppermute(block, XZC, swap_x_with_zc(k)))
    got = jnp.stack(got)
    all_got = [got]
    for r in (1, 3, 2):
        got, early = tie(got, early)
        early = xor_y(got, r)
        all_got.append(early)
    got = jnp.stack([all_got[0], all_got[1], all_got[3], all_got[2]])
    lhs, extra, h = first_build(me, got, other_core(got))


    def cross(send):
        return [send[0]] + [xor_x(send[r], r) for r in (1, 2, 3)]

    def gather(h):
        pieces = [h] + [xor_y(h, r) for r in (1, 2, 3)]
        return pieces + [other_core(p) for p in pieces]

    parts = cross(first_product(me, lhs, extra, w[0], 0))
    sums = parts
    second = first_product(me, lhs, extra, w[1], 1)
    h0 = first_update(h, parts, sums, 0)
    h0, second = tie(h0, second)
    pieces = gather(h0)
    h1 = first_update(h, cross(second), sums, 1)
    lhs, extra, h = second_build(me, pieces + gather(h1))

    h = h.reshape(2 * HALF, WIDE)
    for _ in range(2, STEPS):
        h = update(h, cross(product(me, lhs, extra, w)))
        pieces = gather(h)
        lhs, extra = build(me, pieces)

    h, _ = tie(h, pieces[2])
    old = rows_by_x(me, h)
    lhs, old = tie(lhs, old)
    old = cross(old)
    blocks = last_update(me, cross(last_product(me, lhs, w)), old)
    got = [blocks[0]]
    for dy, dz in ((0, 1), (1, 0), (1, 1)):
        perm = [(i, i ^ (dy * 2 + dz)) for i in range(4)]
        got.append(lax.ppermute(blocks[dy * 2 + dz], ("yh", "z0"), perm))
    return place(me, got + [other_core(g[1]) for g in got])[None]


def solution(mesh):
    fine = Mesh(mesh.devices.reshape(SIZES), AXES)
    group = AXES[:4]
    in_specs = (P(AXES, None), P(group, None, AXES[4:]), P())
    out_specs = P(group, None, AXES[4:])
    return jax.shard_map(per_device, mesh=fine, in_specs=in_specs, out_specs=out_specs, check_vma=False)
```

```python
import functools

import jax
import jax.numpy as jnp
from jax import lax
from jax.experimental import pallas as pl
from jax.experimental.pallas import tpu as pltpu
from jax.sharding import Mesh, PartitionSpec as P

D = 8192
EPS = 1e-06
NX, NZ = 4, 8
HALF = 256
WIDE = 256
AXES = ("yh", "x", "zh", "z0", "yl", "c")
SIZES = (2, 4, 4, 2, 2, 2)
Y = ("yh", "yl")
Z = ("zh", "z0")
YC = ("yh", "yl", "c")
XZC = ("x", "z0", "c")
BF = jnp.bfloat16
F32 = jnp.float32
VMEM = pl.BlockSpec(memory_space=pltpu.VMEM)
SMEM = pl.BlockSpec(memory_space=pltpu.SMEM)
PARAMS = pltpu.CompilerParams(vmem_limit_bytes=12 << 20)


def xor_y(value, r):
    return lax.ppermute(value, Y, [(i, i ^ r) for i in range(4)])


def xor_x(value, r):
    return lax.ppermute(value, "x", [(i, i ^ r) for i in range(4)])


def ring_z(value, step):
    return lax.ppermute(value, Z, [(i, (i + step) % NZ) for i in range(NZ)])


def tie(a, b):
    return lax.optimization_barrier((a, b))


def other_core(value):
    return lax.ppermute(value, "c", [(0, 1), (1, 0)])


def cut_kernel(at_ref, master, gain, out, column):
    row = gain[pl.ds(at_ref[0], 1), :]
    column[...] = jnp.transpose(jnp.broadcast_to(row, (128, 128)))
    scale = column[pl.ds(pl.multiple_of(at_ref[1], 32), 32), :]
    scale = jnp.concatenate([scale, scale], axis=1)
    for b12 in range(2):
        for xx in range(NX):
            for b9 in range(2):
                for b8 in range(2):
                    f = b12 * 4096 + xx * 1024 + b9 * 512 + b8 * 256
                    value = (master[:, f : f + 256].astype(BF).astype(F32) * scale).astype(BF)
                    out[b9 * 4 + b12 * 2 + b8, :, xx * 128 : (xx + 1) * 128] = value[:, :128]
                    out[b9 * 4 + b12 * 2 + b8, :, 512 + xx * 128 : 512 + (xx + 1) * 128] = value[:, 128:]


def cut(at, master, gain):
    return pl.pallas_call(
        cut_kernel,
        out_shape=jax.ShapeDtypeStruct((8, 32, 1024), BF),
        in_specs=[SMEM, VMEM, VMEM],
        out_specs=VMEM,
        scratch_shapes=[pltpu.VMEM((128, 128), F32)],
        compiler_params=PARAMS,
        name="cut",
    )(at, master, gain.reshape(64, 128))


def squares_to_rows(sums):
    row = []
    for j in range(2):
        tile = jnp.transpose(sums[j * 128 : (j + 1) * 128])
        row.append(jnp.broadcast_to(jnp.sum(tile, axis=0, keepdims=True), (16, 128)))
    row = jnp.concatenate(row, axis=1)
    upper = row.astype(BF).astype(F32)
    at = lax.broadcasted_iota(jnp.int32, (16, 256), 0)
    return jnp.where(at < 8, upper, row - upper).astype(BF)


def lane_sums(value):
    wide = value.astype(F32)
    wide = wide * wide
    total = wide[:, 0:128]
    for j in range(1, value.shape[1] // 128):
        total = total + wide[:, j * 128 : (j + 1) * 128]
    return total


def build_kernel(me_ref, *refs):
    pieces, lhs, extra, sums = refs[:8], refs[8], refs[9], refs[10]
    yl, yh, c = me_ref[0], me_ref[1], me_ref[2]
    for half in range(2):
        rows = slice(half * HALF, (half + 1) * HALF)
        total = jnp.zeros((HALF, 128), F32)
        for i, piece in enumerate(pieces):
            r, far = i % 4, i // 4
            at = (yh ^ (r >> 1)) * 512 + (c ^ far) * 256
            value = piece[rows, :]
            lhs[half, yl ^ (r & 1), :, pl.ds(pl.multiple_of(at, 256), 256)] = value
            total = total + lane_sums(value)
        sums[...] = total
        extra[half] = squares_to_rows(sums[...])


def build(me, pieces):
    return pl.pallas_call(
        build_kernel,
        out_shape=[jax.ShapeDtypeStruct((2, 2, HALF, 1024), BF), jax.ShapeDtypeStruct((2, 16, WIDE), BF)],
        in_specs=[SMEM] + [VMEM] * 8,
        out_specs=[VMEM, VMEM],
        scratch_shapes=[pltpu.VMEM((HALF, 128), F32)],
        compiler_params=PARAMS,
        name="build",
    )(me, *pieces)


def first_build_kernel(me_ref, own, other, lhs, extra, h, sums):
    yl, yh, c, z0 = me_ref[0], me_ref[1], me_ref[2], me_ref[4]
    for r in range(4):
        for far, piece in enumerate((own, other)):
            for k in range(4):
                at = (yh ^ (r >> 1)) * 128 + (((c ^ far) * 2 + z0) ^ k) * 32
                lhs[c ^ far, yl ^ (r & 1), pl.ds(pl.multiple_of(at, 32), 32), :] = piece[r, k]
    for m in range(2):
        sums[...] = lane_sums(lhs[m, 0]) + lane_sums(lhs[m, 1])
        extra[m] = squares_to_rows(sums[...])
        h[m] = lhs[m, yl, :, pl.ds(pl.multiple_of(yh * 512 + c * 256, 256), 256)]


def first_build(me, own, other):
    return pl.pallas_call(
        first_build_kernel,
        out_shape=[
            jax.ShapeDtypeStruct((2, 2, HALF, 1024), BF),
            jax.ShapeDtypeStruct((2, 16, WIDE), BF),
            jax.ShapeDtypeStruct((2, HALF, WIDE), BF),
        ],
        in_specs=[SMEM, VMEM, VMEM],
        out_specs=[VMEM, VMEM, VMEM],
        scratch_shapes=[pltpu.VMEM((HALF, 128), F32)],
        compiler_params=PARAMS,
        name="first_build",
    )(me, own, other)


def multiply(left, right, w):
    part = jnp.dot(left, w[:1024, :], preferred_element_type=F32)
    return part + jnp.dot(right, w[1024:, :], preferred_element_type=F32)


def first_product_kernel(me_ref, lhs, extra, w, *refs):
    outs, full = refs[:4], refs[4]
    for half in range(2):
        full[...] = multiply(lhs[half, 0], lhs[half, 1], w)
        for r in range(4):
            cols = pl.ds(pl.multiple_of((me_ref[3] ^ r) * 128, 128), 128)
            outs[r][half * HALF : (half + 1) * HALF, :] = full[:, cols].astype(BF)
    if outs[0].shape[0] > 2 * HALF:
        for r in range(4):
            for half in range(2):
                for j in range(2):
                    at = 2 * HALF + half * 32 + j * 16
                    outs[r][at : at + 16, :] = extra[half, :, j * 128 : (j + 1) * 128]


def first_product(me, lhs, extra, w, n):
    return pl.pallas_call(
        first_product_kernel,
        out_shape=[jax.ShapeDtypeStruct((2 * HALF + (0 if n else 64), 128), BF)] * 4,
        in_specs=[SMEM] + [VMEM] * 3,
        out_specs=[VMEM] * 4,
        scratch_shapes=[pltpu.VMEM((HALF, 512), F32)],
        compiler_params=PARAMS,
        cost_estimate=pl.CostEstimate(flops=1, bytes_accessed=1, transcendentals=0),
        name="first_product",
    )(me, lhs, extra, w)


def first_update_kernel(n, h, *refs):
    parts, sums, out = refs[:4], refs[4:8], refs[8]
    for half in range(2):
        for j in range(2):
            rows = slice(half * HALF + j * 128, half * HALF + (j + 1) * 128)
            at = 2 * HALF + half * 32 + j * 16
            square = jnp.zeros((8, 128), F32)
            for part in sums:
                extra = part[at : at + 16, :].astype(F32)
                square = square + extra[0:8] + extra[8:16]
            scale = lax.rsqrt(jnp.transpose(jnp.broadcast_to(square[0:1], (128, 128))) * (1.0 / D) + EPS)
            total = parts[0][rows, :].astype(F32) + parts[1][rows, :].astype(F32)
            total = total + (parts[2][rows, :].astype(F32) + parts[3][rows, :].astype(F32))
            old = h[half, j * 128 : (j + 1) * 128, n * 128 : (n + 1) * 128].astype(F32)
            out[rows, :] = (old + scale * total).astype(BF)


def first_update(h, parts, sums, n):
    return pl.pallas_call(
        functools.partial(first_update_kernel, n),
        out_shape=jax.ShapeDtypeStruct((2 * HALF, 128), BF),
        in_specs=[VMEM] * 9,
        out_specs=VMEM,
        compiler_params=PARAMS,
        name="first_update",
    )(h, *parts, *sums)


def second_build_kernel(me_ref, *refs):
    pieces, lhs, extra, h, sums = refs[:16], refs[16], refs[17], refs[18], refs[19]
    yl, yh, c = me_ref[0], me_ref[1], me_ref[2]
    for half in range(2):
        rows = slice(half * HALF, (half + 1) * HALF)
        total = jnp.zeros((HALF, 128), F32)
        for i, piece in enumerate(pieces):
            n, far, r = i // 8, i // 4 % 2, i % 4
            at = (yh ^ (r >> 1)) * 512 + (c ^ far) * 256 + n * 128
            value = piece[rows, :]
            lhs[half, yl ^ (r & 1), :, pl.ds(pl.multiple_of(at, 128), 128)] = value
            total = total + lane_sums(value)
            if i % 8 == 0:
                h[half, :, n * 128 : (n + 1) * 128] = value
        sums[...] = total
        extra[half] = squares_to_rows(sums[...])


def second_build(me, pieces):
    return pl.pallas_call(
        second_build_kernel,
        out_shape=[
            jax.ShapeDtypeStruct((2, 2, HALF, 1024), BF),
            jax.ShapeDtypeStruct((2, 16, WIDE), BF),
            jax.ShapeDtypeStruct((2, HALF, WIDE), BF),
        ],
        in_specs=[SMEM] + [VMEM] * 16,
        out_specs=[VMEM] * 3,
        scratch_shapes=[pltpu.VMEM((HALF, 128), F32)],
        compiler_params=PARAMS,
        name="second_build",
    )(me, *pieces)


def product_kernel(r, me_ref, lhs, extra, w0, w1, out):
    cols = pl.ds(pl.multiple_of((me_ref[3] ^ r) * 128, 128), 128)
    both = [jnp.concatenate([w0[k : k + 1024, cols], w1[k : k + 1024, cols]], axis=1) for k in (0, 1024)]
    for half in range(2):
        part = jnp.dot(lhs[half, 0], both[0], preferred_element_type=F32)
        part = part + jnp.dot(lhs[half, 1], both[1], preferred_element_type=F32)
        out[half * HALF : (half + 1) * HALF, :] = part.astype(BF)
        out[2 * HALF + half * 16 : 2 * HALF + half * 16 + 16, :] = extra[half]


def product(me, lhs, extra, w):
    outs = {}
    for r in (2, 1, 3, 0):
        outs[r] = pl.pallas_call(
            functools.partial(product_kernel, r),
            out_shape=jax.ShapeDtypeStruct((2 * HALF + 32, WIDE), BF),
            in_specs=[SMEM] + [VMEM] * 4,
            out_specs=VMEM,
            compiler_params=PARAMS,
            cost_estimate=pl.CostEstimate(flops=1, bytes_accessed=1, transcendentals=0),
            name="product",
        )(me, lhs, extra, *w)
    return outs


def last_product_kernel(me_ref, lhs, h, w0, w1, *refs):
    outs, full, sums = refs[:4], refs[4], refs[5]
    for half in range(2):
        for n, w in enumerate((w0, w1)):
            full[half, :, n * 512 : (n + 1) * 512] = multiply(lhs[half, 0], lhs[half, 1], w).astype(BF)
        sums[half] = lane_sums(lhs[half, 0]) + lane_sums(lhs[half, 1])
    for r in (2, 1, 3, 0):
        squares = []
        for m in range(2):
            for half in range(2):
                rows = pl.ds(pl.multiple_of(m * 128 + (me_ref[3] ^ r) * 32, 32), 32)
                at = m * 64 + half * 32
                outs[r][at : at + 32, :] = full[half, rows, :]
                squares.append(sums[half, rows, :])
                j = m * 2 + half
                outs[r][144:176, j * WIDE : (j + 1) * WIDE] = h[half, rows, :]
        tile = jnp.transpose(jnp.concatenate(squares, axis=0))
        row = jnp.broadcast_to(jnp.sum(tile, axis=0, keepdims=True), (16, 128))
        upper = row.astype(BF).astype(F32)
        at = lax.broadcasted_iota(jnp.int32, (16, 128), 0)
        outs[r][128:144, 0:128] = jnp.where(at < 8, upper, row - upper).astype(BF)
        outs[r][128:144, 128:1024] = jnp.zeros((16, 896), BF)


def last_product(me, lhs, h, w):
    return pl.pallas_call(
        last_product_kernel,
        out_shape=[jax.ShapeDtypeStruct((176, 1024), BF)] * 4,
        in_specs=[SMEM] + [VMEM] * 4,
        out_specs=[VMEM] * 4,
        scratch_shapes=[pltpu.VMEM((2, HALF, 1024), BF), pltpu.VMEM((2, HALF, 128), F32)],
        compiler_params=PARAMS,
        cost_estimate=pl.CostEstimate(flops=1, bytes_accessed=1, transcendentals=0),
        name="last_product",
    )(me, lhs, h, *w)


def scale_of(parts, at, lane):
    square = jnp.zeros((8, 128), F32)
    for part in parts:
        extra = part[at : at + 16, lane : lane + 128].astype(F32)
        square = square + extra[0:8] + extra[8:16]
    return lax.rsqrt(jnp.transpose(jnp.broadcast_to(square[0:1], (128, 128))) * (1.0 / D) + EPS)


def add_up(parts, rows, cols):
    total = parts[0][rows, cols].astype(F32) + parts[1][rows, cols].astype(F32)
    return total + (parts[2][rows, cols].astype(F32) + parts[3][rows, cols].astype(F32))


def update_kernel(h, p0, p1, p2, p3, out):
    parts = (p0, p1, p2, p3)
    for j in range(4):
        rows = slice(j * 128, (j + 1) * 128)
        scale = scale_of(parts, 2 * HALF + (j // 2) * 16, (j % 2) * 128)
        for n in range(2):
            cols = slice(n * 128, (n + 1) * 128)
            out[rows, cols] = (h[rows, cols].astype(F32) + scale * add_up(parts, rows, cols)).astype(BF)


def update(h, parts):
    return pl.pallas_call(
        update_kernel,
        out_shape=jax.ShapeDtypeStruct((2 * HALF, WIDE), BF),
        in_specs=[VMEM] * 5,
        out_specs=VMEM,
        compiler_params=PARAMS,
        name="update",
    )(h, *parts)


def last_update_kernel(me_ref, *refs):
    parts, outs = refs[:4], refs[4]
    yh, c, x, z0 = me_ref[1], me_ref[2], me_ref[3], me_ref[4]
    scale = scale_of(parts, 128, 0)
    for r in range(4):
        xx = x ^ r
        for n in range(2):
            cols = pl.ds(pl.multiple_of(n * 512 + xx * 128, 128), 128)
            value = scale * add_up(parts, slice(0, 128), cols)
            for m in range(2):
                to = (m ^ yh) * 2 + ((xx & 1) ^ z0)
                for half in range(2):
                    at = (m * 2 + half) * WIDE + n * 128
                    old = parts[r][144:176, at : at + 128].astype(F32)
                    new = old + value[m * 64 + half * 32 : m * 64 + half * 32 + 32]
                    outs[to, (xx >> 1) ^ c, half * 32 : half * 32 + 32, n * 128 : (n + 1) * 128] = new.astype(BF)


def last_update(me, parts):
    return pl.pallas_call(
        last_update_kernel,
        out_shape=jax.ShapeDtypeStruct((4, 2, 64, WIDE), BF),
        in_specs=[SMEM] + [VMEM] * 4,
        out_specs=VMEM,
        compiler_params=PARAMS,
        name="last_update",
    )(me, *parts)


def place_kernel(me_ref, *refs):
    out = refs[8]
    yh, c, z0 = me_ref[1], me_ref[2], me_ref[4]
    for i, block in enumerate(refs[:8]):
        far, dy, dz = i // 4, i // 2 % 2, i % 2
        row = pl.ds(pl.multiple_of((z0 ^ dz) * 64, 64), 64)
        col = pl.ds(pl.multiple_of((yh ^ dy) * 512 + (c ^ far) * 256, 256), 256)
        out[row, col] = block[0] if far == 0 else block[...]


def place(me, blocks):
    return pl.pallas_call(
        place_kernel,
        out_shape=jax.ShapeDtypeStruct((128, 1024), BF),
        in_specs=[SMEM] + [VMEM] * 8,
        out_specs=VMEM,
        compiler_params=PARAMS,
        name="place",
    )(me, *blocks)


def swap_x_with_zc(k):
    perm = []
    for i in range(16):
        x, z0, c = i >> 2, (i >> 1) & 1, i & 1
        v = x ^ k
        perm.append((i, (c * 2 + z0) * 4 + (v & 1) * 2 + (v >> 1)))
    return perm


def per_device(master, states, norm_gain):
    yh, x, zh, z0, yl, c = (lax.axis_index(a).astype(jnp.int32) for a in AXES)
    z = zh * 2 + z0
    mine = c * 2 + z0
    me = jnp.stack([yl, yh, c, x, z0])
    row_block = (((yh * NX + x) * NZ + z) * 2 + yl) * 2 + c

    send = cut(jnp.stack([row_block // 4, row_block % 4 * 32]), master, norm_gain)
    own = lax.all_to_all(send, YC, split_axis=0, concat_axis=0, tiled=True).reshape(256, 1024)
    w, early = [], None
    for n in range(2):
        piece = own[:, n * 512 : (n + 1) * 512]
        buf = jnp.zeros((2, NZ, 128, 512), BF)

        def put(buf, piece, at, part=0):
            return lax.dynamic_update_slice(buf, piece.reshape(-1, 1, 128, 512), (part, at % NZ, 0, 0))

        buf = put(buf, piece, z)
        right = left = piece
        for d in range(1, 4):
            right, left = ring_z(right, 1), ring_z(left, -1)
            early = right if early is None else early
            buf = put(buf, right, z - d + NZ)
            buf = put(buf, left, z + d)
        buf = put(buf, ring_z(right[:128], 1), z + 4, 0)
        buf = put(buf, ring_z(left[128:], -1), z + 4, 1)
        w.append(buf.reshape(2048, 512))

    local = states[0].reshape(2, 2, 32, 1024)
    got = []
    for k in range(4):
        v = x ^ k
        block = lax.dynamic_slice(local, (v & 1, v >> 1, 0, 0), (1, 1, 32, 1024))[0, 0]
        got.append(lax.ppermute(block, XZC, swap_x_with_zc(k)))
    got = jnp.stack(got)
    all_got = [got]
    for r in (1, 3, 2):
        got, early = tie(got, early)
        early = xor_y(got, r)
        all_got.append(early)
    got = jnp.stack([all_got[0], all_got[1], all_got[3], all_got[2]])
    lhs, extra, h = first_build(me, got, other_core(got))


    def cross(send):
        return [send[0]] + [xor_x(send[r], r) for r in (1, 2, 3)]

    def gather(h):
        pieces = [h] + [xor_y(h, r) for r in (1, 2, 3)]
        return pieces + [other_core(p) for p in pieces]

    parts = cross(first_product(me, lhs, extra, w[0], 0))
    sums = parts
    second = first_product(me, lhs, extra, w[1], 1)
    h0 = first_update(h, parts, sums, 0)
    h0, second = tie(h0, second)
    pieces = gather(h0)
    h1 = first_update(h, cross(second), sums, 1)
    lhs, extra, h = second_build(me, pieces + gather(h1))

    h = h.reshape(2 * HALF, WIDE)
    h = update(h, cross(product(me, lhs, extra, w)))

    lhs, extra = build(me, gather(h))
    blocks = last_update(me, cross(last_product(me, lhs, h.reshape(2, HALF, WIDE), w)))
    got = [blocks[0]]
    for dy, dz in ((0, 1), (1, 0), (1, 1)):
        perm = [(i, i ^ (dy * 2 + dz)) for i in range(4)]
        got.append(lax.ppermute(blocks[dy * 2 + dz], ("yh", "z0"), perm))
    return place(me, got + [other_core(g[1]) for g in got])[None]


def solution(mesh):
    fine = Mesh(mesh.devices.reshape(SIZES), AXES)
    group = AXES[:4]
    in_specs = (P(AXES, None), P(group, None, AXES[4:]), P())
    out_specs = P(group, None, AXES[4:])
    return jax.shard_map(per_device, mesh=fine, in_specs=in_specs, out_specs=out_specs, check_vma=False)
```

```python
import functools

import jax
import jax.numpy as jnp
from jax import lax
from jax.experimental import pallas as pl
from jax.experimental.pallas import tpu as pltpu
from jax.sharding import Mesh, PartitionSpec as P

D = 8192
EPS = 1e-06
NX, NZ = 4, 8
HALF = 256
WIDE = 256
AXES = ("yh", "x", "zh", "z0", "yl", "c")
SIZES = (2, 4, 4, 2, 2, 2)
Y = ("yh", "yl")
Z = ("zh", "z0")
YC = ("yh", "yl", "c")
XZC = ("x", "z0", "c")
BF = jnp.bfloat16
F32 = jnp.float32
VMEM = pl.BlockSpec(memory_space=pltpu.VMEM)
SMEM = pl.BlockSpec(memory_space=pltpu.SMEM)
PARAMS = pltpu.CompilerParams(vmem_limit_bytes=12 << 20)


def xor_y(value, r):
    return lax.ppermute(value, Y, [(i, i ^ r) for i in range(4)])


def xor_x(value, r):
    return lax.ppermute(value, "x", [(i, i ^ r) for i in range(4)])


def ring_z(value, step):
    return lax.ppermute(value, Z, [(i, (i + step) % NZ) for i in range(NZ)])


def tie(a, b):
    return lax.optimization_barrier((a, b))


def other_core(value):
    return lax.ppermute(value, "c", [(0, 1), (1, 0)])


def cut_kernel(at_ref, master, gain, out, column):
    row = gain[pl.ds(at_ref[0], 1), :]
    column[...] = jnp.transpose(jnp.broadcast_to(row, (128, 128)))
    scale = column[pl.ds(pl.multiple_of(at_ref[1], 32), 32), :]
    scale = jnp.concatenate([scale, scale], axis=1)
    for b12 in range(2):
        for xx in range(NX):
            for b9 in range(2):
                for b8 in range(2):
                    f = b12 * 4096 + xx * 1024 + b9 * 512 + b8 * 256
                    value = (master[:, f : f + 256].astype(BF).astype(F32) * scale).astype(BF)
                    out[b9 * 4 + b12 * 2 + b8, :, xx * 128 : (xx + 1) * 128] = value[:, :128]
                    out[b9 * 4 + b12 * 2 + b8, :, 512 + xx * 128 : 512 + (xx + 1) * 128] = value[:, 128:]


def cut(at, master, gain):
    return pl.pallas_call(
        cut_kernel,
        out_shape=jax.ShapeDtypeStruct((8, 32, 1024), BF),
        in_specs=[SMEM, VMEM, VMEM],
        out_specs=VMEM,
        scratch_shapes=[pltpu.VMEM((128, 128), F32)],
        compiler_params=PARAMS,
        name="cut",
    )(at, master, gain.reshape(64, 128))


def squares_to_rows(sums):
    row = []
    for j in range(2):
        tile = jnp.transpose(sums[j * 128 : (j + 1) * 128])
        row.append(jnp.broadcast_to(jnp.sum(tile, axis=0, keepdims=True), (16, 128)))
    row = jnp.concatenate(row, axis=1)
    upper = row.astype(BF).astype(F32)
    at = lax.broadcasted_iota(jnp.int32, (16, 256), 0)
    return jnp.where(at < 8, upper, row - upper).astype(BF)


def lane_sums(value):
    wide = value.astype(F32)
    wide = wide * wide
    total = wide[:, 0:128]
    for j in range(1, value.shape[1] // 128):
        total = total + wide[:, j * 128 : (j + 1) * 128]
    return total


def build_kernel(me_ref, *refs):
    pieces, lhs, extra, sums = refs[:8], refs[8], refs[9], refs[10]
    yl, yh, c = me_ref[0], me_ref[1], me_ref[2]
    for half in range(2):
        rows = slice(half * HALF, (half + 1) * HALF)
        total = jnp.zeros((HALF, 128), F32)
        for i, piece in enumerate(pieces):
            r, far = i % 4, i // 4
            at = (yh ^ (r >> 1)) * 512 + (c ^ far) * 256
            value = piece[rows, :]
            lhs[half, yl ^ (r & 1), :, pl.ds(pl.multiple_of(at, 256), 256)] = value
            total = total + lane_sums(value)
        sums[...] = total
        extra[half] = squares_to_rows(sums[...])


def build(me, pieces):
    return pl.pallas_call(
        build_kernel,
        out_shape=[jax.ShapeDtypeStruct((2, 2, HALF, 1024), BF), jax.ShapeDtypeStruct((2, 16, WIDE), BF)],
        in_specs=[SMEM] + [VMEM] * 8,
        out_specs=[VMEM, VMEM],
        scratch_shapes=[pltpu.VMEM((HALF, 128), F32)],
        compiler_params=PARAMS,
        name="build",
    )(me, *pieces)


def first_build_kernel(me_ref, own, other, lhs, extra, h, sums):
    yl, yh, c, z0 = me_ref[0], me_ref[1], me_ref[2], me_ref[4]
    for r in range(4):
        for far, piece in enumerate((own, other)):
            for k in range(4):
                at = (yh ^ (r >> 1)) * 128 + (((c ^ far) * 2 + z0) ^ k) * 32
                lhs[c ^ far, yl ^ (r & 1), pl.ds(pl.multiple_of(at, 32), 32), :] = piece[r, k]
    for m in range(2):
        sums[...] = lane_sums(lhs[m, 0]) + lane_sums(lhs[m, 1])
        extra[m] = squares_to_rows(sums[...])
        h[m] = lhs[m, yl, :, pl.ds(pl.multiple_of(yh * 512 + c * 256, 256), 256)]


def first_build(me, own, other):
    return pl.pallas_call(
        first_build_kernel,
        out_shape=[
            jax.ShapeDtypeStruct((2, 2, HALF, 1024), BF),
            jax.ShapeDtypeStruct((2, 16, WIDE), BF),
            jax.ShapeDtypeStruct((2, HALF, WIDE), BF),
        ],
        in_specs=[SMEM, VMEM, VMEM],
        out_specs=[VMEM, VMEM, VMEM],
        scratch_shapes=[pltpu.VMEM((HALF, 128), F32)],
        compiler_params=PARAMS,
        name="first_build",
    )(me, own, other)


def multiply(left, right, w):
    part = jnp.dot(left, w[:1024, :], preferred_element_type=F32)
    return part + jnp.dot(right, w[1024:, :], preferred_element_type=F32)


def first_product_kernel(me_ref, lhs, extra, w, *refs):
    outs, full = refs[:4], refs[4]
    for half in range(2):
        full[...] = multiply(lhs[half, 0], lhs[half, 1], w)
        for r in range(4):
            cols = pl.ds(pl.multiple_of((me_ref[3] ^ r) * 128, 128), 128)
            outs[r][half * HALF : (half + 1) * HALF, :] = full[:, cols].astype(BF)
    if outs[0].shape[0] > 2 * HALF:
        for r in range(4):
            for half in range(2):
                for j in range(2):
                    at = 2 * HALF + half * 32 + j * 16
                    outs[r][at : at + 16, :] = extra[half, :, j * 128 : (j + 1) * 128]


def first_product(me, lhs, extra, w, n):
    return pl.pallas_call(
        first_product_kernel,
        out_shape=[jax.ShapeDtypeStruct((2 * HALF + (0 if n else 64), 128), BF)] * 4,
        in_specs=[SMEM] + [VMEM] * 3,
        out_specs=[VMEM] * 4,
        scratch_shapes=[pltpu.VMEM((HALF, 512), F32)],
        compiler_params=PARAMS,
        cost_estimate=pl.CostEstimate(flops=1, bytes_accessed=1, transcendentals=0),
        name="first_product",
    )(me, lhs, extra, w)


def first_update_kernel(n, h, *refs):
    parts, sums, out = refs[:4], refs[4:8], refs[8]
    for half in range(2):
        for j in range(2):
            rows = slice(half * HALF + j * 128, half * HALF + (j + 1) * 128)
            at = 2 * HALF + half * 32 + j * 16
            square = jnp.zeros((8, 128), F32)
            for part in sums:
                extra = part[at : at + 16, :].astype(F32)
                square = square + extra[0:8] + extra[8:16]
            scale = lax.rsqrt(jnp.transpose(jnp.broadcast_to(square[0:1], (128, 128))) * (1.0 / D) + EPS)
            total = parts[0][rows, :].astype(F32) + parts[1][rows, :].astype(F32)
            total = total + (parts[2][rows, :].astype(F32) + parts[3][rows, :].astype(F32))
            old = h[half, j * 128 : (j + 1) * 128, n * 128 : (n + 1) * 128].astype(F32)
            out[rows, :] = (old + scale * total).astype(BF)


def first_update(h, parts, sums, n):
    return pl.pallas_call(
        functools.partial(first_update_kernel, n),
        out_shape=jax.ShapeDtypeStruct((2 * HALF, 128), BF),
        in_specs=[VMEM] * 9,
        out_specs=VMEM,
        compiler_params=PARAMS,
        name="first_update",
    )(h, *parts, *sums)


def second_build_kernel(me_ref, *refs):
    pieces, lhs, extra, h, sums = refs[:16], refs[16], refs[17], refs[18], refs[19]
    yl, yh, c = me_ref[0], me_ref[1], me_ref[2]
    for half in range(2):
        rows = slice(half * HALF, (half + 1) * HALF)
        total = jnp.zeros((HALF, 128), F32)
        for i, piece in enumerate(pieces):
            n, far, r = i // 8, i // 4 % 2, i % 4
            at = (yh ^ (r >> 1)) * 512 + (c ^ far) * 256 + n * 128
            value = piece[rows, :]
            lhs[half, yl ^ (r & 1), :, pl.ds(pl.multiple_of(at, 128), 128)] = value
            total = total + lane_sums(value)
            if i % 8 == 0:
                h[half, :, n * 128 : (n + 1) * 128] = value
        sums[...] = total
        extra[half] = squares_to_rows(sums[...])


def second_build(me, pieces):
    return pl.pallas_call(
        second_build_kernel,
        out_shape=[
            jax.ShapeDtypeStruct((2, 2, HALF, 1024), BF),
            jax.ShapeDtypeStruct((2, 16, WIDE), BF),
            jax.ShapeDtypeStruct((2, HALF, WIDE), BF),
        ],
        in_specs=[SMEM] + [VMEM] * 16,
        out_specs=[VMEM] * 3,
        scratch_shapes=[pltpu.VMEM((HALF, 128), F32)],
        compiler_params=PARAMS,
        name="second_build",
    )(me, *pieces)


def product_kernel(r, me_ref, lhs, extra, w0, w1, out):
    cols = pl.ds(pl.multiple_of((me_ref[3] ^ r) * 128, 128), 128)
    both = [jnp.concatenate([w0[k : k + 1024, cols], w1[k : k + 1024, cols]], axis=1) for k in (0, 1024)]
    for half in range(2):
        part = jnp.dot(lhs[half, 0], both[0], preferred_element_type=F32)
        part = part + jnp.dot(lhs[half, 1], both[1], preferred_element_type=F32)
        out[half * HALF : (half + 1) * HALF, :] = part.astype(BF)
        out[2 * HALF + half * 16 : 2 * HALF + half * 16 + 16, :] = extra[half]


def product(me, lhs, extra, w):
    outs = {}
    for r in (2, 1, 3, 0):
        outs[r] = pl.pallas_call(
            functools.partial(product_kernel, r),
            out_shape=jax.ShapeDtypeStruct((2 * HALF + 32, WIDE), BF),
            in_specs=[SMEM] + [VMEM] * 4,
            out_specs=VMEM,
            compiler_params=PARAMS,
            cost_estimate=pl.CostEstimate(flops=1, bytes_accessed=1, transcendentals=0),
            name="product",
        )(me, lhs, extra, *w)
    return outs


def last_product_kernel(r, me_ref, lhs, h, w0, w1, out):
    pieces = []
    for m in range(2):
        rows = pl.ds(pl.multiple_of(m * 128 + (me_ref[3] ^ r) * 32, 32), 32)
        for half in range(2):
            pieces.append([lhs[half, b12, rows, :] for b12 in range(2)])
            j = m * 2 + half
            out[144:176, j * WIDE : (j + 1) * WIDE] = h[half, rows, :]
    left, right = (jnp.concatenate([p[b12] for p in pieces], axis=0) for b12 in range(2))
    for n, w in enumerate((w0, w1)):
        out[0:128, n * 512 : (n + 1) * 512] = multiply(left, right, w).astype(BF)
    tile = jnp.transpose(lane_sums(left) + lane_sums(right))
    row = jnp.broadcast_to(jnp.sum(tile, axis=0, keepdims=True), (16, 128))
    upper = row.astype(BF).astype(F32)
    at = lax.broadcasted_iota(jnp.int32, (16, 128), 0)
    out[128:144, 0:128] = jnp.where(at < 8, upper, row - upper).astype(BF)
    out[128:144, 128:1024] = jnp.zeros((16, 896), BF)


def last_product(me, lhs, h, w):
    outs = {}
    for r in (2, 1, 3, 0):
        outs[r] = pl.pallas_call(
            functools.partial(last_product_kernel, r),
            out_shape=jax.ShapeDtypeStruct((176, 1024), BF),
            in_specs=[SMEM] + [VMEM] * 4,
            out_specs=VMEM,
            compiler_params=PARAMS,
            cost_estimate=pl.CostEstimate(flops=1, bytes_accessed=1, transcendentals=0),
            name="last_product",
        )(me, lhs, h, *w)
    return outs


def scale_of(parts, at, lane):
    square = jnp.zeros((8, 128), F32)
    for part in parts:
        extra = part[at : at + 16, lane : lane + 128].astype(F32)
        square = square + extra[0:8] + extra[8:16]
    return lax.rsqrt(jnp.transpose(jnp.broadcast_to(square[0:1], (128, 128))) * (1.0 / D) + EPS)


def add_up(parts, rows, cols):
    total = parts[0][rows, cols].astype(F32) + parts[1][rows, cols].astype(F32)
    return total + (parts[2][rows, cols].astype(F32) + parts[3][rows, cols].astype(F32))


def update_kernel(h, p0, p1, p2, p3, out):
    parts = (p0, p1, p2, p3)
    for j in range(4):
        rows = slice(j * 128, (j + 1) * 128)
        scale = scale_of(parts, 2 * HALF + (j // 2) * 16, (j % 2) * 128)
        for n in range(2):
            cols = slice(n * 128, (n + 1) * 128)
            out[rows, cols] = (h[rows, cols].astype(F32) + scale * add_up(parts, rows, cols)).astype(BF)


def update(h, parts):
    return pl.pallas_call(
        update_kernel,
        out_shape=jax.ShapeDtypeStruct((2 * HALF, WIDE), BF),
        in_specs=[VMEM] * 5,
        out_specs=VMEM,
        compiler_params=PARAMS,
        name="update",
    )(h, *parts)


def last_update_kernel(me_ref, *refs):
    parts, outs = refs[:4], refs[4]
    yh, c, x, z0 = me_ref[1], me_ref[2], me_ref[3], me_ref[4]
    scale = scale_of(parts, 128, 0)
    for r in range(4):
        xx = x ^ r
        for n in range(2):
            cols = pl.ds(pl.multiple_of(n * 512 + xx * 128, 128), 128)
            value = scale * add_up(parts, slice(0, 128), cols)
            for m in range(2):
                to = (m ^ yh) * 2 + ((xx & 1) ^ z0)
                for half in range(2):
                    at = (m * 2 + half) * WIDE + n * 128
                    old = parts[r][144:176, at : at + 128].astype(F32)
                    new = old + value[m * 64 + half * 32 : m * 64 + half * 32 + 32]
                    outs[to, (xx >> 1) ^ c, half * 32 : half * 32 + 32, n * 128 : (n + 1) * 128] = new.astype(BF)


def last_update(me, parts):
    return pl.pallas_call(
        last_update_kernel,
        out_shape=jax.ShapeDtypeStruct((4, 2, 64, WIDE), BF),
        in_specs=[SMEM] + [VMEM] * 4,
        out_specs=VMEM,
        compiler_params=PARAMS,
        name="last_update",
    )(me, *parts)


def place_kernel(me_ref, *refs):
    out = refs[8]
    yh, c, z0 = me_ref[1], me_ref[2], me_ref[4]
    for i, block in enumerate(refs[:8]):
        far, dy, dz = i // 4, i // 2 % 2, i % 2
        row = pl.ds(pl.multiple_of((z0 ^ dz) * 64, 64), 64)
        col = pl.ds(pl.multiple_of((yh ^ dy) * 512 + (c ^ far) * 256, 256), 256)
        out[row, col] = block[0] if far == 0 else block[...]


def place(me, blocks):
    return pl.pallas_call(
        place_kernel,
        out_shape=jax.ShapeDtypeStruct((128, 1024), BF),
        in_specs=[SMEM] + [VMEM] * 8,
        out_specs=VMEM,
        compiler_params=PARAMS,
        name="place",
    )(me, *blocks)


def swap_x_with_zc(k):
    perm = []
    for i in range(16):
        x, z0, c = i >> 2, (i >> 1) & 1, i & 1
        v = x ^ k
        perm.append((i, (c * 2 + z0) * 4 + (v & 1) * 2 + (v >> 1)))
    return perm


def per_device(master, states, norm_gain):
    yh, x, zh, z0, yl, c = (lax.axis_index(a).astype(jnp.int32) for a in AXES)
    z = zh * 2 + z0
    mine = c * 2 + z0
    me = jnp.stack([yl, yh, c, x, z0])
    row_block = (((yh * NX + x) * NZ + z) * 2 + yl) * 2 + c

    send = cut(jnp.stack([row_block // 4, row_block % 4 * 32]), master, norm_gain)
    own = lax.all_to_all(send, YC, split_axis=0, concat_axis=0, tiled=True).reshape(256, 1024)
    w, early = [], None
    for n in range(2):
        piece = own[:, n * 512 : (n + 1) * 512]
        buf = jnp.zeros((2, NZ, 128, 512), BF)

        def put(buf, piece, at, part=0):
            return lax.dynamic_update_slice(buf, piece.reshape(-1, 1, 128, 512), (part, at % NZ, 0, 0))

        buf = put(buf, piece, z)
        right = left = piece
        for d in range(1, 4):
            right, left = ring_z(right, 1), ring_z(left, -1)
            early = right if early is None else early
            buf = put(buf, right, z - d + NZ)
            buf = put(buf, left, z + d)
        buf = put(buf, ring_z(right[:128], 1), z + 4, 0)
        buf = put(buf, ring_z(left[128:], -1), z + 4, 1)
        w.append(buf.reshape(2048, 512))

    local = states[0].reshape(2, 2, 32, 1024)
    got = []
    for k in range(4):
        v = x ^ k
        block = lax.dynamic_slice(local, (v & 1, v >> 1, 0, 0), (1, 1, 32, 1024))[0, 0]
        got.append(lax.ppermute(block, XZC, swap_x_with_zc(k)))
    got = jnp.stack(got)
    all_got = [got]
    for r in (1, 3, 2):
        got, early = tie(got, early)
        early = xor_y(got, r)
        all_got.append(early)
    got = jnp.stack([all_got[0], all_got[1], all_got[3], all_got[2]])
    lhs, extra, h = first_build(me, got, other_core(got))


    def cross(send):
        return [send[0]] + [xor_x(send[r], r) for r in (1, 2, 3)]

    def gather(h):
        pieces = [h] + [xor_y(h, r) for r in (1, 2, 3)]
        return pieces + [other_core(p) for p in pieces]

    parts = cross(first_product(me, lhs, extra, w[0], 0))
    sums = parts
    second = first_product(me, lhs, extra, w[1], 1)
    h0 = first_update(h, parts, sums, 0)
    h0, second = tie(h0, second)
    pieces = gather(h0)
    h1 = first_update(h, cross(second), sums, 1)
    lhs, extra, h = second_build(me, pieces + gather(h1))

    h = h.reshape(2 * HALF, WIDE)
    h = update(h, cross(product(me, lhs, extra, w)))

    lhs, extra = build(me, gather(h))
    blocks = last_update(me, cross(last_product(me, lhs, h.reshape(2, HALF, WIDE), w)))
    got = [blocks[0]]
    for dy, dz in ((0, 1), (1, 0), (1, 1)):
        perm = [(i, i ^ (dy * 2 + dz)) for i in range(4)]
        got.append(lax.ppermute(blocks[dy * 2 + dz], ("yh", "z0"), perm))
    return place(me, got + [other_core(g[1]) for g in got])[None]


def solution(mesh):
    fine = Mesh(mesh.devices.reshape(SIZES), AXES)
    group = AXES[:4]
    in_specs = (P(AXES, None), P(group, None, AXES[4:]), P())
    out_specs = P(group, None, AXES[4:])
    return jax.shard_map(per_device, mesh=fine, in_specs=in_specs, out_specs=out_specs, check_vma=False)
```

```python
import functools

import jax
import jax.numpy as jnp
from jax import lax
from jax.experimental import pallas as pl
from jax.experimental.pallas import tpu as pltpu
from jax.sharding import Mesh, PartitionSpec as P

D = 8192
EPS = 1e-06
NX, NZ = 4, 8
HALF = 256
WIDE = 256
AXES = ("yh", "x", "zh", "z0", "yl", "c")
SIZES = (2, 4, 4, 2, 2, 2)
Y = ("yh", "yl")
Z = ("zh", "z0")
YC = ("yh", "yl", "c")
XZC = ("x", "z0", "c")
BF = jnp.bfloat16
F32 = jnp.float32
VMEM = pl.BlockSpec(memory_space=pltpu.VMEM)
SMEM = pl.BlockSpec(memory_space=pltpu.SMEM)
PARAMS = pltpu.CompilerParams(vmem_limit_bytes=12 << 20)


def xor_y(value, r):
    return lax.ppermute(value, Y, [(i, i ^ r) for i in range(4)])


def xor_x(value, r):
    return lax.ppermute(value, "x", [(i, i ^ r) for i in range(4)])


def ring_z(value, step):
    return lax.ppermute(value, Z, [(i, (i + step) % NZ) for i in range(NZ)])


def tie(a, b):
    return lax.optimization_barrier((a, b))


def other_core(value):
    return lax.ppermute(value, "c", [(0, 1), (1, 0)])


def cut_kernel(at_ref, master, gain, out, column):
    row = gain[pl.ds(at_ref[0], 1), :]
    column[...] = jnp.transpose(jnp.broadcast_to(row, (128, 128)))
    scale = column[pl.ds(pl.multiple_of(at_ref[1], 32), 32), :]
    scale = jnp.concatenate([scale, scale], axis=1)
    for b12 in range(2):
        for xx in range(NX):
            for b9 in range(2):
                for b8 in range(2):
                    f = b12 * 4096 + xx * 1024 + b9 * 512 + b8 * 256
                    value = (master[:, f : f + 256].astype(BF).astype(F32) * scale).astype(BF)
                    out[b9 * 4 + b12 * 2 + b8, :, xx * 128 : (xx + 1) * 128] = value[:, :128]
                    out[b9 * 4 + b12 * 2 + b8, :, 512 + xx * 128 : 512 + (xx + 1) * 128] = value[:, 128:]


def cut(at, master, gain):
    return pl.pallas_call(
        cut_kernel,
        out_shape=jax.ShapeDtypeStruct((8, 32, 1024), BF),
        in_specs=[SMEM, VMEM, VMEM],
        out_specs=VMEM,
        scratch_shapes=[pltpu.VMEM((128, 128), F32)],
        compiler_params=PARAMS,
        name="cut",
    )(at, master, gain.reshape(64, 128))


def squares_to_rows(sums):
    row = []
    for j in range(2):
        tile = jnp.transpose(sums[j * 128 : (j + 1) * 128])
        row.append(jnp.broadcast_to(jnp.sum(tile, axis=0, keepdims=True), (16, 128)))
    row = jnp.concatenate(row, axis=1)
    upper = row.astype(BF).astype(F32)
    at = lax.broadcasted_iota(jnp.int32, (16, 256), 0)
    return jnp.where(at < 8, upper, row - upper).astype(BF)


def lane_sums(value):
    wide = value.astype(F32)
    wide = wide * wide
    total = wide[:, 0:128]
    for j in range(1, value.shape[1] // 128):
        total = total + wide[:, j * 128 : (j + 1) * 128]
    return total


def build_kernel(me_ref, *refs):
    pieces, lhs, extra, sums = refs[:8], refs[8], refs[9], refs[10]
    yl, yh, c = me_ref[0], me_ref[1], me_ref[2]
    for half in range(2):
        rows = slice(half * HALF, (half + 1) * HALF)
        total = jnp.zeros((HALF, 128), F32)
        for i, piece in enumerate(pieces):
            r, far = i % 4, i // 4
            at = (yh ^ (r >> 1)) * 512 + (c ^ far) * 256
            value = piece[rows, :]
            lhs[half, yl ^ (r & 1), :, pl.ds(pl.multiple_of(at, 256), 256)] = value
            total = total + lane_sums(value)
        sums[...] = total
        extra[half] = squares_to_rows(sums[...])


def build(me, pieces):
    return pl.pallas_call(
        build_kernel,
        out_shape=[jax.ShapeDtypeStruct((2, 2, HALF, 1024), BF), jax.ShapeDtypeStruct((2, 16, WIDE), BF)],
        in_specs=[SMEM] + [VMEM] * 8,
        out_specs=[VMEM, VMEM],
        scratch_shapes=[pltpu.VMEM((HALF, 128), F32)],
        compiler_params=PARAMS,
        name="build",
    )(me, *pieces)


def first_build_kernel(me_ref, own, other, lhs, extra, h, sums):
    yl, yh, c, z0 = me_ref[0], me_ref[1], me_ref[2], me_ref[4]
    for r in range(4):
        for far, piece in enumerate((own, other)):
            for k in range(4):
                at = (yh ^ (r >> 1)) * 128 + (((c ^ far) * 2 + z0) ^ k) * 32
                lhs[c ^ far, yl ^ (r & 1), pl.ds(pl.multiple_of(at, 32), 32), :] = piece[r, k]
    for m in range(2):
        sums[...] = lane_sums(lhs[m, 0]) + lane_sums(lhs[m, 1])
        extra[m] = squares_to_rows(sums[...])
        h[m] = lhs[m, yl, :, pl.ds(pl.multiple_of(yh * 512 + c * 256, 256), 256)]


def first_build(me, own, other):
    return pl.pallas_call(
        first_build_kernel,
        out_shape=[
            jax.ShapeDtypeStruct((2, 2, HALF, 1024), BF),
            jax.ShapeDtypeStruct((2, 16, WIDE), BF),
            jax.ShapeDtypeStruct((2, HALF, WIDE), BF),
        ],
        in_specs=[SMEM, VMEM, VMEM],
        out_specs=[VMEM, VMEM, VMEM],
        scratch_shapes=[pltpu.VMEM((HALF, 128), F32)],
        compiler_params=PARAMS,
        name="first_build",
    )(me, own, other)


def multiply(left, right, w):
    part = jnp.dot(left, w[:1024, :], preferred_element_type=F32)
    return part + jnp.dot(right, w[1024:, :], preferred_element_type=F32)


def first_product_kernel(me_ref, lhs, extra, w, *refs):
    outs, full = refs[:4], refs[4]
    for half in range(2):
        full[...] = multiply(lhs[half, 0], lhs[half, 1], w)
        for r in range(4):
            cols = pl.ds(pl.multiple_of((me_ref[3] ^ r) * 128, 128), 128)
            outs[r][half * HALF : (half + 1) * HALF, :] = full[:, cols].astype(BF)
    if outs[0].shape[0] > 2 * HALF:
        for r in range(4):
            for half in range(2):
                for j in range(2):
                    at = 2 * HALF + half * 32 + j * 16
                    outs[r][at : at + 16, :] = extra[half, :, j * 128 : (j + 1) * 128]


def first_product(me, lhs, extra, w, n):
    return pl.pallas_call(
        first_product_kernel,
        out_shape=[jax.ShapeDtypeStruct((2 * HALF + (0 if n else 64), 128), BF)] * 4,
        in_specs=[SMEM] + [VMEM] * 3,
        out_specs=[VMEM] * 4,
        scratch_shapes=[pltpu.VMEM((HALF, 512), F32)],
        compiler_params=PARAMS,
        cost_estimate=pl.CostEstimate(flops=1, bytes_accessed=1, transcendentals=0),
        name="first_product",
    )(me, lhs, extra, w)


def first_update_kernel(n, h, *refs):
    parts, sums, out = refs[:4], refs[4:8], refs[8]
    for half in range(2):
        for j in range(2):
            rows = slice(half * HALF + j * 128, half * HALF + (j + 1) * 128)
            at = 2 * HALF + half * 32 + j * 16
            square = jnp.zeros((8, 128), F32)
            for part in sums:
                extra = part[at : at + 16, :].astype(F32)
                square = square + extra[0:8] + extra[8:16]
            scale = lax.rsqrt(jnp.transpose(jnp.broadcast_to(square[0:1], (128, 128))) * (1.0 / D) + EPS)
            total = parts[0][rows, :].astype(F32) + parts[1][rows, :].astype(F32)
            total = total + (parts[2][rows, :].astype(F32) + parts[3][rows, :].astype(F32))
            old = h[half, j * 128 : (j + 1) * 128, n * 128 : (n + 1) * 128].astype(F32)
            out[rows, :] = (old + scale * total).astype(BF)


def first_update(h, parts, sums, n):
    return pl.pallas_call(
        functools.partial(first_update_kernel, n),
        out_shape=jax.ShapeDtypeStruct((2 * HALF, 128), BF),
        in_specs=[VMEM] * 9,
        out_specs=VMEM,
        compiler_params=PARAMS,
        name="first_update",
    )(h, *parts, *sums)


def second_build_kernel(me_ref, *refs):
    pieces, lhs, extra, h, sums = refs[:16], refs[16], refs[17], refs[18], refs[19]
    yl, yh, c = me_ref[0], me_ref[1], me_ref[2]
    for half in range(2):
        rows = slice(half * HALF, (half + 1) * HALF)
        total = jnp.zeros((HALF, 128), F32)
        for i, piece in enumerate(pieces):
            n, far, r = i // 8, i // 4 % 2, i % 4
            at = (yh ^ (r >> 1)) * 512 + (c ^ far) * 256 + n * 128
            value = piece[rows, :]
            lhs[half, yl ^ (r & 1), :, pl.ds(pl.multiple_of(at, 128), 128)] = value
            total = total + lane_sums(value)
            if i % 8 == 0:
                h[half, :, n * 128 : (n + 1) * 128] = value
        sums[...] = total
        extra[half] = squares_to_rows(sums[...])


def second_build(me, pieces):
    return pl.pallas_call(
        second_build_kernel,
        out_shape=[
            jax.ShapeDtypeStruct((2, 2, HALF, 1024), BF),
            jax.ShapeDtypeStruct((2, 16, WIDE), BF),
            jax.ShapeDtypeStruct((2, HALF, WIDE), BF),
        ],
        in_specs=[SMEM] + [VMEM] * 16,
        out_specs=[VMEM] * 3,
        scratch_shapes=[pltpu.VMEM((HALF, 128), F32)],
        compiler_params=PARAMS,
        name="second_build",
    )(me, *pieces)


def product_kernel(r, me_ref, lhs, extra, w0, w1, out):
    cols = pl.ds(pl.multiple_of((me_ref[3] ^ r) * 128, 128), 128)
    both = [jnp.concatenate([w0[k : k + 1024, cols], w1[k : k + 1024, cols]], axis=1) for k in (0, 1024)]
    for half in range(2):
        part = jnp.dot(lhs[half, 0], both[0], preferred_element_type=F32)
        part = part + jnp.dot(lhs[half, 1], both[1], preferred_element_type=F32)
        out[half * HALF : (half + 1) * HALF, :] = part.astype(BF)
        out[2 * HALF + half * 16 : 2 * HALF + half * 16 + 16, :] = extra[half]


def product(me, lhs, extra, w):
    outs = {}
    for r in (2, 1, 3, 0):
        outs[r] = pl.pallas_call(
            functools.partial(product_kernel, r),
            out_shape=jax.ShapeDtypeStruct((2 * HALF + 32, WIDE), BF),
            in_specs=[SMEM] + [VMEM] * 4,
            out_specs=VMEM,
            compiler_params=PARAMS,
            cost_estimate=pl.CostEstimate(flops=1, bytes_accessed=1, transcendentals=0),
            name="product",
        )(me, lhs, extra, *w)
    return outs


def last_product_kernel(r, me_ref, lhs, h, w0, w1, out):
    pieces = []
    for m in range(2):
        rows = pl.ds(pl.multiple_of(m * 128 + (me_ref[3] ^ r) * 32, 32), 32)
        for half in range(2):
            pieces.append([lhs[half, b12, rows, :] for b12 in range(2)])
            at = 512 + m * 64 + half * 32
            out[at : at + 32, :] = h[half, rows, :]
    left, right = (jnp.concatenate([p[b12] for p in pieces], axis=0) for b12 in range(2))
    for n, w in enumerate((w0, w1)):
        part = multiply(left, right, w).astype(BF)
        for xx in range(NX):
            out[xx * 128 : (xx + 1) * 128, n * 128 : (n + 1) * 128] = part[:, xx * 128 : (xx + 1) * 128]
    tile = jnp.transpose(lane_sums(left) + lane_sums(right))
    row = jnp.broadcast_to(jnp.sum(tile, axis=0, keepdims=True), (16, 128))
    upper = row.astype(BF).astype(F32)
    at = lax.broadcasted_iota(jnp.int32, (16, 128), 0)
    out[640:656, 0:128] = jnp.where(at < 8, upper, row - upper).astype(BF)
    out[640:656, 128:256] = jnp.zeros((16, 128), BF)


def last_product(me, lhs, h, w):
    outs = {}
    for r in (2, 1, 3, 0):
        outs[r] = pl.pallas_call(
            functools.partial(last_product_kernel, r),
            out_shape=jax.ShapeDtypeStruct((656, WIDE), BF),
            in_specs=[SMEM] + [VMEM] * 4,
            out_specs=VMEM,
            compiler_params=PARAMS,
            cost_estimate=pl.CostEstimate(flops=1, bytes_accessed=1, transcendentals=0),
            name="last_product",
        )(me, lhs, h, *w)
    return outs


def scale_of(parts, at, lane):
    square = jnp.zeros((8, 128), F32)
    for part in parts:
        extra = part[at : at + 16, lane : lane + 128].astype(F32)
        square = square + extra[0:8] + extra[8:16]
    return lax.rsqrt(jnp.transpose(jnp.broadcast_to(square[0:1], (128, 128))) * (1.0 / D) + EPS)


def add_up(parts, rows, cols):
    total = parts[0][rows, cols].astype(F32) + parts[1][rows, cols].astype(F32)
    return total + (parts[2][rows, cols].astype(F32) + parts[3][rows, cols].astype(F32))


def update_kernel(h, p0, p1, p2, p3, out):
    parts = (p0, p1, p2, p3)
    for j in range(4):
        rows = slice(j * 128, (j + 1) * 128)
        scale = scale_of(parts, 2 * HALF + (j // 2) * 16, (j % 2) * 128)
        for n in range(2):
            cols = slice(n * 128, (n + 1) * 128)
            out[rows, cols] = (h[rows, cols].astype(F32) + scale * add_up(parts, rows, cols)).astype(BF)


def update(h, parts):
    return pl.pallas_call(
        update_kernel,
        out_shape=jax.ShapeDtypeStruct((2 * HALF, WIDE), BF),
        in_specs=[VMEM] * 5,
        out_specs=VMEM,
        compiler_params=PARAMS,
        name="update",
    )(h, *parts)


def last_update_kernel(me_ref, *refs):
    parts, outs = refs[:4], refs[4]
    yh, c, x, z0 = me_ref[1], me_ref[2], me_ref[3], me_ref[4]
    scale = scale_of(parts, 640, 0)
    for r in range(4):
        xx = x ^ r
        for n in range(2):
            cols = slice(n * 128, (n + 1) * 128)
            value = scale * add_up(parts, pl.ds(pl.multiple_of(xx * 128, 128), 128), cols)
            for m in range(2):
                to = (m ^ yh) * 2 + ((xx & 1) ^ z0)
                for half in range(2):
                    at = 512 + m * 64 + half * 32
                    old = parts[r][at : at + 32, cols].astype(F32)
                    new = old + value[m * 64 + half * 32 : m * 64 + half * 32 + 32]
                    outs[to, (xx >> 1) ^ c, half * 32 : half * 32 + 32, n * 128 : (n + 1) * 128] = new.astype(BF)


def last_update(me, parts):
    return pl.pallas_call(
        last_update_kernel,
        out_shape=jax.ShapeDtypeStruct((4, 2, 64, WIDE), BF),
        in_specs=[SMEM] + [VMEM] * 4,
        out_specs=VMEM,
        compiler_params=PARAMS,
        name="last_update",
    )(me, *parts)


def place_kernel(me_ref, *refs):
    out = refs[8]
    yh, c, z0 = me_ref[1], me_ref[2], me_ref[4]
    for i, block in enumerate(refs[:8]):
        far, dy, dz = i // 4, i // 2 % 2, i % 2
        row = pl.ds(pl.multiple_of((z0 ^ dz) * 64, 64), 64)
        col = pl.ds(pl.multiple_of((yh ^ dy) * 512 + (c ^ far) * 256, 256), 256)
        out[row, col] = block[0] if far == 0 else block[...]


def place(me, blocks):
    return pl.pallas_call(
        place_kernel,
        out_shape=jax.ShapeDtypeStruct((128, 1024), BF),
        in_specs=[SMEM] + [VMEM] * 8,
        out_specs=VMEM,
        compiler_params=PARAMS,
        name="place",
    )(me, *blocks)


def swap_x_with_zc(k):
    perm = []
    for i in range(16):
        x, z0, c = i >> 2, (i >> 1) & 1, i & 1
        v = x ^ k
        perm.append((i, (c * 2 + z0) * 4 + (v & 1) * 2 + (v >> 1)))
    return perm


def per_device(master, states, norm_gain):
    yh, x, zh, z0, yl, c = (lax.axis_index(a).astype(jnp.int32) for a in AXES)
    z = zh * 2 + z0
    mine = c * 2 + z0
    me = jnp.stack([yl, yh, c, x, z0])
    row_block = (((yh * NX + x) * NZ + z) * 2 + yl) * 2 + c

    send = cut(jnp.stack([row_block // 4, row_block % 4 * 32]), master, norm_gain)
    own = lax.all_to_all(send, YC, split_axis=0, concat_axis=0, tiled=True).reshape(256, 1024)
    w, early = [], None
    for n in range(2):
        piece = own[:, n * 512 : (n + 1) * 512]
        buf = jnp.zeros((2, NZ, 128, 512), BF)

        def put(buf, piece, at, part=0):
            return lax.dynamic_update_slice(buf, piece.reshape(-1, 1, 128, 512), (part, at % NZ, 0, 0))

        buf = put(buf, piece, z)
        right = left = piece
        for d in range(1, 4):
            right, left = ring_z(right, 1), ring_z(left, -1)
            early = right if early is None else early
            buf = put(buf, right, z - d + NZ)
            buf = put(buf, left, z + d)
        buf = put(buf, ring_z(right[:128], 1), z + 4, 0)
        buf = put(buf, ring_z(left[128:], -1), z + 4, 1)
        w.append(buf.reshape(2048, 512))

    local = states[0].reshape(2, 2, 32, 1024)
    got = []
    for k in range(4):
        v = x ^ k
        block = lax.dynamic_slice(local, (v & 1, v >> 1, 0, 0), (1, 1, 32, 1024))[0, 0]
        got.append(lax.ppermute(block, XZC, swap_x_with_zc(k)))
    got = jnp.stack(got)
    all_got = [got]
    for r in (1, 3, 2):
        got, early = tie(got, early)
        early = xor_y(got, r)
        all_got.append(early)
    got = jnp.stack([all_got[0], all_got[1], all_got[3], all_got[2]])
    lhs, extra, h = first_build(me, got, other_core(got))


    def cross(send):
        return [send[0]] + [xor_x(send[r], r) for r in (1, 2, 3)]

    def gather(h):
        pieces = [h] + [xor_y(h, r) for r in (1, 2, 3)]
        return pieces + [other_core(p) for p in pieces]

    parts = cross(first_product(me, lhs, extra, w[0], 0))
    sums = parts
    second = first_product(me, lhs, extra, w[1], 1)
    h0 = first_update(h, parts, sums, 0)
    h0, second = tie(h0, second)
    pieces = gather(h0)
    h1 = first_update(h, cross(second), sums, 1)
    lhs, extra, h = second_build(me, pieces + gather(h1))

    h = h.reshape(2 * HALF, WIDE)
    h = update(h, cross(product(me, lhs, extra, w)))

    lhs, extra = build(me, gather(h))
    blocks = last_update(me, cross(last_product(me, lhs, h.reshape(2, HALF, WIDE), w)))
    got = [blocks[0]]
    for dy, dz in ((0, 1), (1, 0), (1, 1)):
        perm = [(i, i ^ (dy * 2 + dz)) for i in range(4)]
        got.append(lax.ppermute(blocks[dy * 2 + dz], ("yh", "z0"), perm))
    return place(me, got + [other_core(g[1]) for g in got])[None]


def solution(mesh):
    fine = Mesh(mesh.devices.reshape(SIZES), AXES)
    group = AXES[:4]
    in_specs = (P(AXES, None), P(group, None, AXES[4:]), P())
    out_specs = P(group, None, AXES[4:])
    return jax.shard_map(per_device, mesh=fine, in_specs=in_specs, out_specs=out_specs, check_vma=False)
```
